256 devices in a mesh: head: 4 (over y), ctx: 64 (over x, z, core).
Axes of the slice: x: 4, y: 4, z: 8, core: 2. Of those that a mesh axis runs over, the one named last changes fastest.
Arguments:
- query: bfloat16 [64, 512, 4096], P('ctx', 'head'), may hold values from -6 to 6
- keys: bfloat16 [64, 512, 4096], P('ctx', 'head'), may hold values from -6 to 6
- values: bfloat16 [64, 512, 4096], P('ctx', 'head'), may hold values from -6 to 6
- grad_out: bfloat16 [64, 512, 4096], P('ctx', 'head'), may hold values from -6 to 6
Outputs:
- grad_q: bfloat16 [64, 512, 4096], P('ctx', None, 'head')
- grad_k: bfloat16 [64, 512, 4096], P('ctx', None, 'head')
- grad_v: bfloat16 [64, 512, 4096], P('ctx', None, 'head')
The draws below stay inside these ranges and needn't reach their ends.
All inputs are finite; a program needn't handle non-finite values.
Results may differ from the reference program's by a relative error of at most 0.0049.
Values may be sent and summed in bfloat16 or wider, within the bound.
A program may use at most 192 MiB of HBM per device.

```python
import jax
import jax.numpy as jnp
from jax import lax

HD = 128
BLOCK = 512
TOK_DEV = 512
HEADS = 32
WIDTH = 4096
SPANS = 64
LENGTH = 32768


def block_scale(own_key, shape, split, low, largest):
    factor_of, own = 1.0, jax.random.fold_in(own_key, 6)
    for axis_at, shards_of in split:
        steps = jnp.exp(jax.random.uniform(jax.random.fold_in(own, axis_at), (shards_of,), jnp.float32, low / len(split), largest / len(split)))
        factor_of = factor_of * jnp.repeat(steps, shape[axis_at] // shards_of).reshape([-1 if axis == axis_at else 1 for axis in range(len(shape))])
    return factor_of


def scatter_about(key, dims, deviation, bound, split=(), held_as=jnp.bfloat16):
    loudness = block_scale(key, dims, split, -0.22, 0.18) if split else 1.0
    values = jax.random.normal(key, dims, jnp.float32) * deviation * loudness
    return jnp.minimum(jnp.maximum(values, -bound), bound).astype(held_as)


def setup_inputs(seed: int = 0) -> dict:
    splits = jax.random.split(jax.random.key(seed), 5)
    return {
        "query": scatter_about(splits[0], (SPANS, TOK_DEV, WIDTH), 1.0, 6.0, ((0, 64), (1, 4))),
        "keys": scatter_about(splits[1], (SPANS, TOK_DEV, WIDTH), 1.0, 6.0, ((0, 64), (1, 4))),
        "values": scatter_about(splits[2], (SPANS, TOK_DEV, WIDTH), 1.0, 6.0, ((0, 64), (1, 4))),
        "grad_out": scatter_about(splits[3], (SPANS, TOK_DEV, WIDTH), 1.0, 6.0, ((0, 64), (1, 4))),
    }


def reference(query, keys, values, grad_out):
    factor = (HD * LENGTH) ** -0.5
    count = LENGTH // BLOCK

    def split_heads(x):
        return x.reshape(count, BLOCK, HEADS, HD)

    query_blocks = split_heads(query)
    keys_blocks = split_heads(keys)
    values_blocks = split_heads(values)
    grads_blocks = split_heads(grad_out)

    def own_states(item):
        qpart, kpart, vpart, gpart = item
        key_part = jnp.einsum('cha,chb->hab', kpart.astype(jnp.float32), vpart.astype(jnp.float32))
        query_part = jnp.einsum('cha,chb->hab', qpart.astype(jnp.float32), gpart.astype(jnp.float32))
        return key_part, query_part

    key_own, query_own = lax.map(own_states, (query_blocks, keys_blocks, values_blocks, grads_blocks))
    key_states = jnp.cumsum(key_own, 0) - key_own
    query_states = jnp.sum(query_own, 0)[None] - jnp.cumsum(query_own, 0)
    causal = jnp.tril(jnp.ones((BLOCK, BLOCK), jnp.bool_))

    def block_grads(item):
        qpart, kpart, vpart, gpart, kstate, qstate = item
        key_rounded = kstate.astype(jnp.bfloat16).astype(jnp.float32)
        query_rounded = qstate.astype(jnp.bfloat16).astype(jnp.float32)
        qf = qpart.astype(jnp.float32)
        kf = kpart.astype(jnp.float32)
        vf = vpart.astype(jnp.float32)
        gf = gpart.astype(jnp.float32)
        out_scores = jnp.einsum('phd,thd->hpt', gf, vf) * factor
        out_scores = jnp.where(causal[None], out_scores, 0.0).astype(jnp.bfloat16).astype(jnp.float32)
        key_scores = jnp.einsum('phd,thd->hpt', qf, kf) * factor
        key_scores = jnp.where(causal[None], key_scores, 0.0).astype(jnp.bfloat16).astype(jnp.float32)
        grad_query = jnp.einsum('hpt,thd->phd', out_scores, kf) + factor * jnp.einsum('phe,hde->phd', gf, key_rounded)
        grad_key = jnp.einsum('hpt,phd->thd', out_scores, qf) + factor * jnp.einsum('the,hde->thd', vf, query_rounded)
        grad_value = jnp.einsum('hpt,phe->the', key_scores, gf) + factor * jnp.einsum('thd,hde->the', kf, query_rounded)
        return grad_query.astype(jnp.bfloat16), grad_key.astype(jnp.bfloat16), grad_value.astype(jnp.bfloat16)

    grad_query, grad_key, grad_value = lax.map(block_grads, (query_blocks, keys_blocks, values_blocks, grads_blocks, key_states, query_states))
    shape = (SPANS, TOK_DEV, WIDTH)
    return grad_query.reshape(shape), grad_key.reshape(shape), grad_value.reshape(shape)
```

```python
import functools

import jax
import jax.numpy as jnp
from jax import lax
from jax.experimental import pallas as pl
from jax.experimental.pallas import tpu as pltpu
from jax.sharding import PartitionSpec as P

HD = 128
BLOCK = 512
HALF = 256
MESH = pl.DeviceIdType.MESH
NT = (((1,), (1,)), ((), ()))
NN = (((1,), (0,)), ((), ()))
TN = (((0,), (0,)), ((), ()))
WINDOW = 8


def dot(a, b, dims):
    return lax.dot_general(a, b, dims, preferred_element_type=jnp.float32)


def kernel(
    heads, nx, row, factor,
    q_in, k_in, v_in, g_in, gq_out, gk_out, gv_out,
    xin, acc, own, gat, tot, pre, st,
    y_send, y_recv, y_loc, a_send, a_recv, b_send, b_recv, c_send, c_recv,
):
    ny = lax.axis_size("head")
    y = lax.axis_index("head")
    ctx = lax.axis_index("ctx")
    x = ctx // row
    me = ctx % row
    is_q = me // (row // 2)
    rows_y = BLOCK // ny
    ins = (q_in, k_in, v_in, g_in)
    per = 2 * HD // row
    dists = (2, 1, 3)

    def row_peer(d):
        t = lax.rem(me + d, row)
        return t, {"ctx": x * row + t}

    def x_peer(d):
        return {"ctx": lax.rem(x + d, nx) * row + me}

    barrier = pltpu.get_barrier_semaphore()
    for d in dists:
        pl.semaphore_signal(barrier, inc=1, device_id={"head": lax.rem(y + d, ny)}, device_id_type=MESH)
    for d in range(1, row):
        pl.semaphore_signal(barrier, inc=1, device_id=row_peer(d)[1], device_id_type=MESH)
    for d in range(1, nx):
        pl.semaphore_signal(barrier, inc=1, device_id=x_peer(d), device_id_type=MESH)
    pl.semaphore_wait(barrier, ny - 1 + row - 1 + nx - 1)

    def my_rows(owner):
        return pl.ds(pl.multiple_of(owner * rows_y, rows_y), rows_y)

    def cols(owner, h):
        return pl.ds(pl.multiple_of((owner * heads + h) * HD, HD), HD)

    def send_y(h):
        for d in dists:
            tgt = lax.rem(y + d, ny)
            for a in range(4):
                pltpu.make_async_remote_copy(
                    src_ref=ins[a].at[0, :, cols(tgt, h)],
                    dst_ref=xin.at[h, a, my_rows(y), :],
                    send_sem=y_send.at[h],
                    recv_sem=y_recv.at[h],
                    device_id={"head": tgt},
                    device_id_type=MESH,
                ).start()
        for a in range(4):
            pltpu.make_async_copy(
                ins[a].at[0, :, cols(y, h)], xin.at[h, a, my_rows(y), :], y_loc.at[h]
            ).start()

    def wait_bytes(ref, sem):
        pltpu.make_async_copy(ref, ref, sem).wait()

    def states(h):
        wait_bytes(xin.at[h, 0 : ny - 1], y_recv.at[h])
        wait_bytes(xin.at[h, 0:1], y_loc.at[h])
        own[h, 0:HD, :] = dot(xin[h, 1], xin[h, 2], TN)
        own[h, HD : 2 * HD, :] = dot(xin[h, 0], xin[h, 3], TN)
        for d in range(1, row):
            t, peer = row_peer(d)
            pltpu.make_async_remote_copy(
                src_ref=own.at[h, pl.ds(pl.multiple_of(t * per, per), per), :],
                dst_ref=gat.at[h, me],
                send_sem=a_send.at[h],
                recv_sem=a_recv.at[h],
                device_id=peer,
                device_id_type=MESH,
            ).start()
        gat[h, me] = own[h, pl.ds(pl.multiple_of(me * per, per), per), :]

    def totals(h):
        wait_bytes(gat.at[h, 0 : row - 1], a_recv.at[h])
        total = gat[h, 0]
        for s in range(1, row):
            total = total + gat[h, s]
        tot[h, x] = total
        for d in range(1, nx):
            pltpu.make_async_remote_copy(
                src_ref=tot.at[h, x],
                dst_ref=tot.at[h, x],
                send_sem=b_send.at[h],
                recv_sem=b_recv.at[h],
                device_id=x_peer(d),
                device_id_type=MESH,
            ).start()

    def prefixes(h):
        wait_bytes(tot.at[h, 0 : nx - 1], b_recv.at[h])
        run = jnp.zeros((per, HD), jnp.float32)
        for s in range(nx):
            before = (s - x) * (2 * is_q - 1) > 0
            run = run + jnp.where(before, tot[h, s], 0.0)
        for s in range(row):
            at = s + is_q * (row - 1 - 2 * s)
            pre[h, at] = run.astype(jnp.bfloat16)
            run = run + gat[h, at]
        for d in range(1, row):
            t, peer = row_peer(d)
            pltpu.make_async_remote_copy(
                src_ref=pre.at[h, t],
                dst_ref=st.at[h, me],
                send_sem=c_send.at[h],
                recv_sem=c_recv.at[h],
                device_id=peer,
                device_id_type=MESH,
            ).start()
        st[h, me] = pre[h, me]

    r_at = lax.broadcasted_iota(jnp.int32, (HALF, HALF), 0)
    c_at = lax.broadcasted_iota(jnp.int32, (HALF, HALF), 1)

    def causal(h):
        lo, hi = pl.ds(0, HALF), pl.ds(HALF, HALF)

        def low(s):
            return jnp.where(r_at >= c_at, s, 0.0).astype(jnp.bfloat16)

        def upp(s):
            return jnp.where(r_at <= c_at, s, 0.0).astype(jnp.bfloat16)

        def part(a, at):
            return xin[h, a, at, :]

        def scores(left, right, first, other, last):
            s_first = dot(part(left, lo), part(right, lo), NT)
            s_last = dot(part(left, hi), part(right, hi), NT)
            s_other = dot(part(left, first), part(right, last), NT)
            return other(s_first), s_other.astype(jnp.bfloat16), other(s_last)

        a00, a10, a11 = scores(3, 2, hi, low, lo)
        acc[h, 0, lo, :] = dot(a00, part(1, lo), NN)
        acc[h, 0, hi, :] = dot(a10, part(1, lo), NN) + dot(a11, part(1, hi), NN)
        t00, t01, t11 = scores(2, 3, lo, upp, hi)
        acc[h, 1, lo, :] = dot(t00, part(0, lo), NN) + dot(t01, part(0, hi), NN)
        acc[h, 1, hi, :] = dot(t11, part(0, hi), NN)
        b00, b01, b11 = scores(1, 0, lo, upp, hi)
        acc[h, 2, lo, :] = dot(b00, part(3, lo), NN) + dot(b01, part(3, hi), NN)
        acc[h, 2, hi, :] = dot(b11, part(3, hi), NN)

    def finish(h):
        wait_bytes(st.at[h, 0 : row - 1], c_recv.at[h])
        ks = st[h, 0 : row // 2].reshape(HD, HD)
        qs = st[h, row // 2 : row].reshape(HD, HD)
        at = pl.ds(pl.multiple_of(h * HD, HD), HD)
        gq_out[0, :, at] = (factor * (acc[h, 0] + dot(xin[h, 3], ks, NT))).astype(jnp.bfloat16)
        gk_out[0, :, at] = (factor * (acc[h, 1] + dot(xin[h, 2], qs, NT))).astype(jnp.bfloat16)
        gv_out[0, :, at] = (factor * (acc[h, 2] + dot(xin[h, 1], qs, NN))).astype(jnp.bfloat16)

    @pl.loop(0, min(WINDOW, heads))
    def _(h):
        send_y(h)

    @pl.loop(0, heads)
    def _(h):
        if WINDOW < heads:
            @pl.when(h + WINDOW < heads)
            def _():
                send_y(h + WINDOW)

        states(h)
        causal(h)

        @pl.when(h >= 1)
        def _():
            totals(h - 1)

        @pl.when(h >= 2)
        def _():
            prefixes(h - 2)

        @pl.when(h >= 3)
        def _():
            finish(h - 3)

    prefixes(heads - 2)
    finish(heads - 3)
    totals(heads - 1)
    finish(heads - 2)
    prefixes(heads - 1)
    finish(heads - 1)

    @pl.loop(0, heads)
    def _(h):
        wait_bytes(xin.at[h, 0 : ny - 1], y_send.at[h])
        wait_bytes(gat.at[h, 0 : row - 1], a_send.at[h])
        wait_bytes(tot.at[h, 0 : nx - 1], b_send.at[h])
        wait_bytes(st.at[h, 0 : row - 1], c_send.at[h])


def shards(nx, query, keys, values, grad_out):
    ny = lax.axis_size("head")
    nctx = lax.axis_size("ctx")
    row = nctx // nx
    heads = query.shape[2] // ny // HD
    factor = (HD * BLOCK * nctx) ** (-0.5)
    per = 2 * HD // row
    dma = pltpu.SemaphoreType.DMA((heads,))
    flops = heads * (9 * 2 * BLOCK * BLOCK * HD * 3 // 4 + 5 * 2 * BLOCK * HD * HD)
    ins = [pltpu.with_memory_space_constraint(a, pltpu.HBM) for a in (query, keys, values, grad_out)]
    return pl.pallas_call(
        functools.partial(kernel, heads, nx, row, factor),
        out_shape=[pltpu.VMEM((1, BLOCK, heads * HD), jnp.bfloat16)] * 3,
        in_specs=[pl.BlockSpec(memory_space=pltpu.HBM)] * 4,
        out_specs=[pl.BlockSpec(memory_space=pltpu.VMEM)] * 3,
        scratch_shapes=[
            pltpu.VMEM((heads, 4, BLOCK, HD), jnp.bfloat16),
            pltpu.VMEM((heads, 3, BLOCK, HD), jnp.float32),
            pltpu.VMEM((heads, 2 * HD, HD), jnp.float32),
            pltpu.VMEM((heads, row, per, HD), jnp.float32),
            pltpu.VMEM((heads, nx, per, HD), jnp.float32),
            pltpu.VMEM((heads, row, per, HD), jnp.bfloat16),
            pltpu.VMEM((heads, row, per, HD), jnp.bfloat16),
        ]
        + [dma] * 9,
        compiler_params=pltpu.CompilerParams(
            collective_id=1, has_side_effects=True, vmem_limit_bytes=40 * 2**20
        ),
        cost_estimate=pl.CostEstimate(flops=flops, bytes_accessed=8 * 2**20, transcendentals=0),
    )(*ins)


def solution(mesh):
    nx = 4
    in_specs = (P("ctx", "head", None),) * 4
    out_specs = (P("ctx", None, "head"),) * 3
    return jax.shard_map(
        functools.partial(shards, nx), mesh=mesh, in_specs=in_specs, out_specs=out_specs, check_vma=False
    )
```

```python
import functools

import jax
import jax.numpy as jnp
from jax import lax
from jax.experimental import pallas as pl
from jax.experimental.pallas import tpu as pltpu
from jax.sharding import PartitionSpec as P

HD = 128
BLOCK = 512
HALF = 256
MESH = pl.DeviceIdType.MESH
NT = (((1,), (1,)), ((), ()))
NN = (((1,), (0,)), ((), ()))
TN = (((0,), (0,)), ((), ()))
WINDOW = 4
BEFORE = 1
EARLY = 3
AT_SUM, AT_TOTAL, AT_PREFIX = 0, 1, 2
LAG_TOTAL, LAG_PREFIX, LAG_FINISH = 1, 2, 3


def dot(a, b, dims):
    return lax.dot_general(a, b, dims, preferred_element_type=jnp.float32)


def kernel(
    heads, nx, row, factor,
    q_in, k_in, v_in, g_in, gq_out, gk_out, gv_out,
    xin, acc, own, gat, tot, pre, st,
    ear, psend, precv, chip, egat, etot, epre, est, mate,
    rounds, y_send, y_recv, y_loc, a_send, a_recv, b_send, b_recv, c_send, c_recv,
    m_send, m_recv, e_loc, e_send, e_recv, p_send, p_recv,
    ea_send, ea_recv, eb_send, eb_recv, ec_send, ec_recv,
):
    ny = lax.axis_size("head")
    y = lax.axis_index("head")
    ctx = lax.axis_index("ctx")
    nz = row // 2
    x = ctx // row
    me = ctx % row
    z = me // 2
    core = me % 2
    is_q = me // nz
    rows_y = BLOCK // ny
    ins = (q_in, k_in, v_in, g_in)
    per = 2 * HD // row
    early = ear.shape[3] // HD
    normal = heads - early
    dists = (2, 1, 3)

    def y_peer(d):
        return {"head": lax.rem(y + d, ny)}

    def place(x_at, z_at, core_at):
        return {"ctx": (x_at * nz + z_at) * 2 + core_at}

    def row_peer(d):
        t = lax.rem(me + d, row)
        return t, {"ctx": x * row + t}

    def x_peer(d):
        return {"ctx": lax.rem(x + d, nx) * row + me}

    partner = place(x, z, 1 - core)
    z_next = [place(x, lax.rem(z + d, nz), core) for d in (1, nz - 1)]
    x_next = [x_peer(d) for d in (1, nx - 1)]
    near = [y_peer(d) for d in dists] + [partner] + z_next + x_next

    def signal(sem, device):
        pl.semaphore_signal(sem, inc=1, device_id=device, device_id_type=MESH)

    barrier = pltpu.get_barrier_semaphore()
    for device in near:
        signal(barrier, device)
    pl.semaphore_wait(barrier, len(near))

    def remote(src, dst, send, recv, device):
        pltpu.make_async_remote_copy(
            src_ref=src, dst_ref=dst, send_sem=send, recv_sem=recv,
            device_id=device, device_id_type=MESH,
        ).start()

    def wait_bytes(ref, sem):
        pltpu.make_async_copy(ref, ref, sem).wait()

    def my_rows(owner):
        return pl.ds(pl.multiple_of(owner * rows_y, rows_y), rows_y)

    def cols(owner, h, count=1):
        return pl.ds(pl.multiple_of((owner * heads + h) * HD, HD), count * HD)

    def send_y(h):
        for d in dists:
            tgt = lax.rem(y + d, ny)
            for a in range(4):
                remote(
                    ins[a].at[0, :, cols(tgt, h)], xin.at[h, a, my_rows(y), :],
                    y_send.at[h], y_recv.at[h], {"head": tgt},
                )
        for a in range(4):
            pltpu.make_async_copy(
                ins[a].at[0, :, cols(y, h)], xin.at[h, a, my_rows(y), :], y_loc.at[h]
            ).start()

    def early_rows():
        at = pl.ds(pl.multiple_of(core * rows_y, rows_y), rows_y)
        keys_side, query_side = (k_in, v_in), (q_in, g_in)

        def go(keep, give):
            for t in range(ny):
                for i in range(2):
                    src = (0, slice(None), cols(t, normal, early))
                    dst = ear.at[i, t, at, :]
                    remote(give[i].at[src], dst, e_send, e_recv, partner)
                    pltpu.make_async_copy(keep[i].at[src], dst, e_loc).start()

        @pl.when(core == 0)
        def _():
            go(keys_side, query_side)

        @pl.when(core == 1)
        def _():
            go(query_side, keys_side)

    def early_parts():
        wait_bytes(ear.at[0], e_loc)
        wait_bytes(ear.at[0], e_recv)
        for d in (2, 1, 3, 0):
            t = lax.rem(y + d, ny)
            for e in range(early):
                at = slice(e * HD, (e + 1) * HD)
                part = dot(ear[0, t, :, at], ear[1, t, :, at], TN)
                if d:
                    psend[d, e] = part.astype(jnp.bfloat16)
                else:
                    chip[:, e] = part.reshape(nz, per, HD)
            if d:
                remote(psend.at[d], precv.at[y], p_send, p_recv, y_peer(d))

    def early_sum():
        wait_bytes(precv.at[0 : ny - 1], p_recv)
        for e in range(early):
            total = chip[:, e]
            for d in range(1, ny):
                got = precv[lax.rem(y + d, ny), e].astype(jnp.float32)
                total = total + got.reshape(nz, per, HD)
            chip[:, e] = total
        for d in range(1, nz):
            t = lax.rem(z + d, nz)
            remote(chip.at[t], egat.at[z], ea_send, ea_recv, place(x, t, core))
        egat[z] = chip[z]

    def early_totals():
        wait_bytes(egat.at[0 : nz - 1], ea_recv)
        total = egat[0]
        for s in range(1, nz):
            total = total + egat[s]
        etot[x] = total
        for d in range(1, nx):
            remote(etot.at[x], etot.at[x], eb_send, eb_recv, x_peer(d))

    def base(parts, x_side):
        run = jnp.zeros(parts.shape[1:], jnp.float32)
        for s in range(nx):
            run = run + jnp.where((s - x) * x_side > 0, parts[s], 0.0)
        return run

    def early_prefixes():
        wait_bytes(etot.at[0 : nx - 1], eb_recv)
        run = base(etot, 2 * core - 1)
        for s in range(nz):
            at = s + core * (nz - 1 - 2 * s)
            epre[at] = run
            run = run + egat[at]
        mine = core * nz + z
        for d in range(1, row):
            t, peer = row_peer(d)
            remote(epre.at[t // 2], est.at[mine], ec_send, ec_recv, peer)
        est[mine] = epre[z]

    def wait_y(h):
        wait_bytes(xin.at[h, 0 : ny - 1], y_recv.at[h])
        wait_bytes(xin.at[h, 0:1], y_loc.at[h])

    def states(h):
        own[h, 0:HD, :] = dot(xin[h, 1], xin[h, 2], TN)
        own[h, HD : 2 * HD, :] = dot(xin[h, 0], xin[h, 3], TN)
        for d in range(1, row):
            t, peer = row_peer(d)
            src = own.at[h, pl.ds(pl.multiple_of(t * per, per), per), :]
            remote(src, gat.at[h, me], a_send.at[h], a_recv.at[h], peer)
        gat[h, me] = own[h, pl.ds(pl.multiple_of(me * per, per), per), :]

    def late_state(h):
        e = h - normal
        mate[0, e] = dot(xin[h, 1 - core], xin[h, 2 + core], TN)
        remote(mate.at[0, e], mate.at[1, e], m_send.at[e], m_recv.at[e], partner)

    def totals(h):
        wait_bytes(gat.at[h, 0 : row - 1], a_recv.at[h])
        total = gat[h, 0]
        for s in range(1, row):
            total = total + gat[h, s]
        tot[h, x] = total
        for d in range(1, nx):
            remote(tot.at[h, x], tot.at[h, x], b_send.at[h], b_recv.at[h], x_peer(d))

    def prefixes(h):
        wait_bytes(tot.at[h, 0 : nx - 1], b_recv.at[h])
        run = base(tot.at[h], 2 * is_q - 1)
        for s in range(row):
            at = s + is_q * (row - 1 - 2 * s)
            pre[h, at] = run.astype(jnp.bfloat16)
            run = run + gat[h, at]
        for d in range(1, row):
            t, peer = row_peer(d)
            remote(pre.at[h, t], st.at[h, me], c_send.at[h], c_recv.at[h], peer)
        st[h, me] = pre[h, me]

    r_at = lax.broadcasted_iota(jnp.int32, (HALF, HALF), 0)
    c_at = lax.broadcasted_iota(jnp.int32, (HALF, HALF), 1)

    def causal(h):
        lo, hi = pl.ds(0, HALF), pl.ds(HALF, HALF)

        def low(s):
            return jnp.where(r_at >= c_at, s, 0.0).astype(jnp.bfloat16)

        def upp(s):
            return jnp.where(r_at <= c_at, s, 0.0).astype(jnp.bfloat16)

        def part(a, at):
            return xin[h, a, at, :]

        def scores(left, right, first, other, last):
            s_first = dot(part(left, lo), part(right, lo), NT)
            s_last = dot(part(left, hi), part(right, hi), NT)
            s_other = dot(part(left, first), part(right, last), NT)
            return other(s_first), s_other.astype(jnp.bfloat16), other(s_last)

        a00, a10, a11 = scores(3, 2, hi, low, lo)
        acc[h, 0, lo, :] = dot(a00, part(1, lo), NN)
        acc[h, 0, hi, :] = dot(a10, part(1, lo), NN) + dot(a11, part(1, hi), NN)
        t00, t01, t11 = scores(2, 3, lo, upp, hi)
        acc[h, 1, lo, :] = dot(t00, part(0, lo), NN) + dot(t01, part(0, hi), NN)
        acc[h, 1, hi, :] = dot(t11, part(0, hi), NN)
        b00, b01, b11 = scores(1, 0, lo, upp, hi)
        acc[h, 2, lo, :] = dot(b00, part(3, lo), NN) + dot(b01, part(3, hi), NN)
        acc[h, 2, hi, :] = dot(b11, part(3, hi), NN)

    def finish(h, ks, qs):
        at = pl.ds(pl.multiple_of(h * HD, HD), HD)
        gq_out[0, :, at] = (factor * (acc[h, 0] + dot(xin[h, 3], ks, NT))).astype(jnp.bfloat16)
        gk_out[0, :, at] = (factor * (acc[h, 1] + dot(xin[h, 2], qs, NT))).astype(jnp.bfloat16)
        gv_out[0, :, at] = (factor * (acc[h, 2] + dot(xin[h, 1], qs, NN))).astype(jnp.bfloat16)

    def finish_normal(h):
        wait_bytes(st.at[h, 0 : row - 1], c_recv.at[h])
        ks = st[h, 0 : row // 2].reshape(HD, HD)
        qs = st[h, row // 2 : row].reshape(HD, HD)
        finish(h, ks, qs)

    def finish_early(h):
        e = h - normal
        wait_bytes(mate.at[0, e], m_recv.at[e])
        late = mate[1, e]
        ks = est[0:nz, e].reshape(HD, HD) + jnp.where(core == 1, late, 0.0)
        qs = est[nz : 2 * nz, e].reshape(HD, HD) + jnp.where(core == 0, late, 0.0)
        finish(h, ks.astype(jnp.bfloat16), qs.astype(jnp.bfloat16))

    for h in range(min(WINDOW, BEFORE)):
        send_y(h)
    early_rows()
    for r in range(rounds.shape[0]):
        for device in z_next + x_next:
            signal(rounds.at[r], device)
        if r == 0:
            early_parts()
            for h in range(BEFORE, min(WINDOW, heads)):
                send_y(h)
        pl.semaphore_wait(rounds.at[r], 4)

    @pl.loop(0, heads)
    def _(h):
        @pl.when(h + WINDOW < heads)
        def _():
            send_y(h + WINDOW)

        wait_y(h)

        @pl.when(h < normal)
        def _():
            states(h)

        @pl.when(h >= normal)
        def _():
            late_state(h)

        @pl.when(h == AT_SUM)
        def _():
            early_sum()

        causal(h)

        def lagged(lag, first, end, fn):
            @pl.when((h - lag >= first) & (h - lag < end))
            def _():
                fn(h - lag)

        lagged(LAG_TOTAL, 0, normal, totals)

        @pl.when(h == AT_TOTAL)
        def _():
            early_totals()

        lagged(LAG_PREFIX, 0, normal, prefixes)

        @pl.when(h == AT_PREFIX)
        def _():
            early_prefixes()

        lagged(LAG_FINISH, 0, normal, finish_normal)

        @pl.when(h == normal)
        def _():
            wait_bytes(est.at[0 : row - 1], ec_recv)

        lagged(1, normal, heads, finish_early)

    finish_early(heads - 1)

    wait_bytes(ear.at[0], e_send)
    wait_bytes(precv.at[0 : ny - 1], p_send)
    wait_bytes(egat.at[0 : nz - 1], ea_send)
    wait_bytes(etot.at[0 : nx - 1], eb_send)
    wait_bytes(est.at[0 : row - 1], ec_send)

    @pl.loop(0, heads)
    def _(h):
        wait_bytes(xin.at[h, 0 : ny - 1], y_send.at[h])

    @pl.loop(0, normal)
    def _(h):
        wait_bytes(gat.at[h, 0 : row - 1], a_send.at[h])
        wait_bytes(tot.at[h, 0 : nx - 1], b_send.at[h])
        wait_bytes(st.at[h, 0 : row - 1], c_send.at[h])

    @pl.loop(0, early)
    def _(e):
        wait_bytes(mate.at[0, e], m_send.at[e])


def shards(nx, query, keys, values, grad_out):
    ny = lax.axis_size("head")
    nctx = lax.axis_size("ctx")
    row = nctx // nx
    nz = row // 2
    heads = query.shape[2] // ny // HD
    factor = (HD * BLOCK * nctx) ** (-0.5)
    per = 2 * HD // row
    early = min(EARLY, heads - 1)
    normal = heads - early
    dma = pltpu.SemaphoreType.DMA
    flops = heads * (9 * 2 * BLOCK * BLOCK * HD * 3 // 4 + 5 * 2 * BLOCK * HD * HD)
    ins = [pltpu.with_memory_space_constraint(a, pltpu.HBM) for a in (query, keys, values, grad_out)]
    f32, bf16 = jnp.float32, jnp.bfloat16
    return pl.pallas_call(
        functools.partial(kernel, heads, nx, row, factor),
        out_shape=[pltpu.VMEM((1, BLOCK, heads * HD), bf16)] * 3,
        in_specs=[pl.BlockSpec(memory_space=pltpu.HBM)] * 4,
        out_specs=[pl.BlockSpec(memory_space=pltpu.VMEM)] * 3,
        scratch_shapes=[
            pltpu.VMEM((heads, 4, BLOCK, HD), bf16),
            pltpu.VMEM((heads, 3, BLOCK, HD), f32),
            pltpu.VMEM((normal, 2 * HD, HD), f32),
            pltpu.VMEM((normal, row, per, HD), f32),
            pltpu.VMEM((normal, nx, per, HD), f32),
            pltpu.VMEM((normal, row, per, HD), bf16),
            pltpu.VMEM((normal, row, per, HD), bf16),
            pltpu.VMEM((2, ny, 2 * BLOCK // ny, early * HD), bf16),
            pltpu.VMEM((ny, early, HD, HD), bf16),
            pltpu.VMEM((ny, early, HD, HD), bf16),
            pltpu.VMEM((nz, early, per, HD), f32),
            pltpu.VMEM((nz, early, per, HD), f32),
            pltpu.VMEM((nx, early, per, HD), f32),
            pltpu.VMEM((nz, early, per, HD), f32),
            pltpu.VMEM((row, early, per, HD), f32),
            pltpu.VMEM((2, early, HD, HD), f32),
            pltpu.SemaphoreType.REGULAR((nz // 2,)),
        ]
        + [dma((heads,))] * 3
        + [dma((normal,))] * 6
        + [dma((early,))] * 2
        + [dma] * 11,
        compiler_params=pltpu.CompilerParams(
            collective_id=1, has_side_effects=True, vmem_limit_bytes=44 * 2**20
        ),
        cost_estimate=pl.CostEstimate(flops=flops, bytes_accessed=8 * 2**20, transcendentals=0),
    )(*ins)


def solution(mesh):
    nx = 4
    in_specs = (P("ctx", "head", None),) * 4
    out_specs = (P("ctx", None, "head"),) * 3
    return jax.shard_map(
        functools.partial(shards, nx), mesh=mesh, in_specs=in_specs, out_specs=out_specs, check_vma=False
    )
```

```python
import functools

import jax
import jax.numpy as jnp
from jax import lax
from jax.experimental import pallas as pl
from jax.experimental.pallas import tpu as pltpu
from jax.sharding import PartitionSpec as P

HD = 128
BLOCK = 512
HALF = 256
MESH = pl.DeviceIdType.MESH
NT = (((1,), (1,)), ((), ()))
NN = (((1,), (0,)), ((), ()))
TN = (((0,), (0,)), ((), ()))
WINDOW = 4
BEFORE = 1
EARLY = 4
AT_SUM, AT_TOTAL, AT_PREFIX, AT_SHARE, AT_FINISH = 0, 1, 2, 5, 6
LAG_TOTAL, LAG_PREFIX, LAG_FINISH = 1, 2, 4


def dot(a, b, dims):
    return lax.dot_general(a, b, dims, preferred_element_type=jnp.float32)


def kernel(
    heads, nx, row, factor,
    q_in, k_in, v_in, g_in, gq_out, gk_out, gv_out,
    xin, acc, own, gat, tot, pre, st,
    ear, psend, precv, chip, egat, etot, epre, est, mate,
    rounds, y_send, y_recv, y_loc, a_send, a_recv, b_send, b_recv, c_send, c_recv,
    m_send, m_recv, e_loc, e_send, e_recv, p_send, p_recv,
    ea_send, ea_recv, eb_send, eb_recv, ec_send, ec_recv, ed_send, ed_recv,
):
    ny = lax.axis_size("head")
    y = lax.axis_index("head")
    ctx = lax.axis_index("ctx")
    nz = row // 2
    x = ctx // row
    me = ctx % row
    z = me // 2
    core = me % 2
    is_q = me // nz
    rows_y = BLOCK // ny
    ins = (q_in, k_in, v_in, g_in)
    per = 2 * HD // row
    early = ear.shape[3] // HD
    normal = heads - early
    dists = (2, 1, 3)

    def y_peer(d):
        return {"head": lax.rem(y + d, ny)}

    def place(x_at, z_at, core_at):
        return {"ctx": (x_at * nz + z_at) * 2 + core_at}

    def row_peer(d):
        t = lax.rem(me + d, row)
        return t, {"ctx": x * row + t}

    def x_peer(d):
        return {"ctx": lax.rem(x + d, nx) * row + me}

    partner = place(x, z, 1 - core)
    near = [y_peer(d) for d in dists] + [partner] + [x_peer(d) for d in (1, nx - 1)]

    def signal(sem, device):
        pl.semaphore_signal(sem, inc=1, device_id=device, device_id_type=MESH)

    def signal_line(sem, step):
        @pl.when(z >= step)
        def _():
            signal(sem, place(x, z - step, core))

        @pl.when(z + step < nz)
        def _():
            signal(sem, place(x, z + step, core))

    def line_count(step):
        return lax.min(z // step, 1) + lax.min((nz - 1 - z) // step, 1)

    barrier = pltpu.get_barrier_semaphore()
    for device in near:
        signal(barrier, device)
    signal_line(barrier, 1)
    pl.semaphore_wait(barrier, len(near) + line_count(1))

    def remote(src, dst, send, recv, device):
        pltpu.make_async_remote_copy(
            src_ref=src, dst_ref=dst, send_sem=send, recv_sem=recv,
            device_id=device, device_id_type=MESH,
        ).start()

    def wait_bytes(ref, sem):
        pltpu.make_async_copy(ref, ref, sem).wait()

    def my_rows(owner):
        return pl.ds(pl.multiple_of(owner * rows_y, rows_y), rows_y)

    def cols(owner, h, count=1):
        return pl.ds(pl.multiple_of((owner * heads + h) * HD, HD), count * HD)

    def send_y(h):
        for d in dists:
            tgt = lax.rem(y + d, ny)
            for a in range(4):
                remote(
                    ins[a].at[0, :, cols(tgt, h)], xin.at[h, a, my_rows(y), :],
                    y_send.at[h], y_recv.at[h], {"head": tgt},
                )
        for a in range(4):
            pltpu.make_async_copy(
                ins[a].at[0, :, cols(y, h)], xin.at[h, a, my_rows(y), :], y_loc.at[h]
            ).start()

    def early_rows():
        at = pl.ds(pl.multiple_of(core * rows_y, rows_y), rows_y)
        keys_side, query_side = (k_in, v_in), (q_in, g_in)

        def go(keep, give):
            for t in range(ny):
                for i in range(2):
                    src = (0, slice(None), cols(t, normal, early))
                    dst = ear.at[i, t, at, :]
                    remote(give[i].at[src], dst, e_send, e_recv, partner)
                    pltpu.make_async_copy(keep[i].at[src], dst, e_loc).start()

        @pl.when(core == 0)
        def _():
            go(keys_side, query_side)

        @pl.when(core == 1)
        def _():
            go(query_side, keys_side)

    def early_parts():
        wait_bytes(ear.at[0], e_loc)
        wait_bytes(ear.at[0], e_recv)
        for d in (2, 1, 3, 0):
            t = lax.rem(y + d, ny)
            for e in range(early):
                at = slice(e * HD, (e + 1) * HD)
                part = dot(ear[0, t, :, at], ear[1, t, :, at], TN)
                if d:
                    psend[d, e] = part.astype(jnp.bfloat16)
                else:
                    chip[:, e] = part.reshape(nz, per, HD)
            if d:
                remote(psend.at[d], precv.at[y], p_send, p_recv, y_peer(d))

    def early_sum():
        wait_bytes(precv.at[0 : ny - 1], p_recv)
        for e in range(early):
            total = chip[:, e]
            for d in range(1, ny):
                got = precv[lax.rem(y + d, ny), e].astype(jnp.float32)
                total = total + got.reshape(nz, per, HD)
            chip[:, e] = total
        for d in range(1, nz):
            t = lax.rem(z + d, nz)
            remote(chip.at[t], egat.at[z], ea_send, ea_recv, place(x, t, core))
        egat[z] = chip[z]

    def early_totals():
        wait_bytes(egat.at[0 : nz - 1], ea_recv)
        total = egat[0]
        for s in range(1, nz):
            total = total + egat[s]
        etot[x] = total
        for d in range(1, nx):
            remote(etot.at[x], etot.at[x], eb_send, eb_recv, x_peer(d))

    def base(parts, x_side):
        run = jnp.zeros(parts.shape[1:], jnp.float32)
        for s in range(nx):
            run = run + jnp.where((s - x) * x_side > 0, parts[s], 0.0)
        return run

    def early_prefixes():
        wait_bytes(etot.at[0 : nx - 1], eb_recv)
        run = base(etot, 2 * core - 1)
        for s in range(nz):
            at = s + core * (nz - 1 - 2 * s)
            epre[at] = run
            run = run + egat[at]
        for d in range(1, nz):
            t = lax.rem(z + d, nz)
            remote(epre.at[t], est.at[core, z], ec_send, ec_recv, place(x, t, core))
        est[core, z] = epre[z]

    def early_share():
        wait_bytes(est.at[0, 0 : nz - 1], ec_recv)
        remote(est.at[core], est.at[core], ed_send, ed_recv, partner)

    def wait_y(h):
        wait_bytes(xin.at[h, 0 : ny - 1], y_recv.at[h])
        wait_bytes(xin.at[h, 0:1], y_loc.at[h])

    def states(h):
        own[h, 0:HD, :] = dot(xin[h, 1], xin[h, 2], TN)
        own[h, HD : 2 * HD, :] = dot(xin[h, 0], xin[h, 3], TN)
        for d in range(1, row):
            t, peer = row_peer(d)
            src = own.at[h, pl.ds(pl.multiple_of(t * per, per), per), :]
            remote(src, gat.at[h, me], a_send.at[h], a_recv.at[h], peer)
        gat[h, me] = own[h, pl.ds(pl.multiple_of(me * per, per), per), :]

    def late_state(h):
        e = h - normal
        mate[0, e] = dot(xin[h, 1 - core], xin[h, 2 + core], TN)
        remote(mate.at[0, e], mate.at[1, e], m_send.at[e], m_recv.at[e], partner)

    def totals(h):
        wait_bytes(gat.at[h, 0 : row - 1], a_recv.at[h])
        total = gat[h, 0]
        for s in range(1, row):
            total = total + gat[h, s]
        tot[h, x] = total
        for d in range(1, nx):
            remote(tot.at[h, x], tot.at[h, x], b_send.at[h], b_recv.at[h], x_peer(d))

    def prefixes(h):
        wait_bytes(tot.at[h, 0 : nx - 1], b_recv.at[h])
        run = base(tot.at[h], 2 * is_q - 1)
        for s in range(row):
            at = s + is_q * (row - 1 - 2 * s)
            pre[h, at] = run.astype(jnp.bfloat16)
            run = run + gat[h, at]
        for d in range(1, row):
            t, peer = row_peer(d)
            remote(pre.at[h, t], st.at[h, me], c_send.at[h], c_recv.at[h], peer)
        st[h, me] = pre[h, me]

    r_at = lax.broadcasted_iota(jnp.int32, (HALF, HALF), 0)
    c_at = lax.broadcasted_iota(jnp.int32, (HALF, HALF), 1)

    def causal(h):
        lo, hi = pl.ds(0, HALF), pl.ds(HALF, HALF)

        def low(s):
            return jnp.where(r_at >= c_at, s, 0.0).astype(jnp.bfloat16)

        def upp(s):
            return jnp.where(r_at <= c_at, s, 0.0).astype(jnp.bfloat16)

        def part(a, at):
            return xin[h, a, at, :]

        def scores(left, right, first, other, last):
            s_first = dot(part(left, lo), part(right, lo), NT)
            s_last = dot(part(left, hi), part(right, hi), NT)
            s_other = dot(part(left, first), part(right, last), NT)
            return other(s_first), s_other.astype(jnp.bfloat16), other(s_last)

        a00, a10, a11 = scores(3, 2, hi, low, lo)
        acc[h, 0, lo, :] = dot(a00, part(1, lo), NN)
        acc[h, 0, hi, :] = dot(a10, part(1, lo), NN) + dot(a11, part(1, hi), NN)
        t00, t01, t11 = scores(2, 3, lo, upp, hi)
        acc[h, 1, lo, :] = dot(t00, part(0, lo), NN) + dot(t01, part(0, hi), NN)
        acc[h, 1, hi, :] = dot(t11, part(0, hi), NN)
        b00, b01, b11 = scores(1, 0, lo, upp, hi)
        acc[h, 2, lo, :] = dot(b00, part(3, lo), NN) + dot(b01, part(3, hi), NN)
        acc[h, 2, hi, :] = dot(b11, part(3, hi), NN)

    def finish(h, ks, qs):
        at = pl.ds(pl.multiple_of(h * HD, HD), HD)
        gq_out[0, :, at] = (factor * (acc[h, 0] + dot(xin[h, 3], ks, NT))).astype(jnp.bfloat16)
        gk_out[0, :, at] = (factor * (acc[h, 1] + dot(xin[h, 2], qs, NT))).astype(jnp.bfloat16)
        gv_out[0, :, at] = (factor * (acc[h, 2] + dot(xin[h, 1], qs, NN))).astype(jnp.bfloat16)

    def finish_normal(h):
        wait_bytes(st.at[h, 0 : row - 1], c_recv.at[h])
        ks = st[h, 0 : row // 2].reshape(HD, HD)
        qs = st[h, row // 2 : row].reshape(HD, HD)
        finish(h, ks, qs)

    def finish_early(h):
        e = h - normal
        wait_bytes(mate.at[0, e], m_recv.at[e])
        late = mate[1, e]
        ks = est[0, :, e].reshape(HD, HD) + jnp.where(core == 1, late, 0.0)
        qs = est[1, :, e].reshape(HD, HD) + jnp.where(core == 0, late, 0.0)
        finish(h, ks.astype(jnp.bfloat16), qs.astype(jnp.bfloat16))

    for h in range(min(WINDOW, BEFORE)):
        send_y(h)
    early_rows()
    for r in range(rounds.shape[0]):
        signal_line(rounds.at[r], 2**r)
        if r == 0:
            for d in (1, nx - 1):
                signal(rounds.at[r], x_peer(d))
            early_parts()
            for h in range(BEFORE, min(WINDOW, heads)):
                send_y(h)
        pl.semaphore_wait(rounds.at[r], line_count(2**r) + (2 if r == 0 else 0))

    @pl.loop(0, heads)
    def _(h):
        @pl.when(h + WINDOW < heads)
        def _():
            send_y(h + WINDOW)

        wait_y(h)

        @pl.when(h < normal)
        def _():
            states(h)

        @pl.when(h >= normal)
        def _():
            late_state(h)

        def lagged(lag, first, end, fn):
            @pl.when((h - lag >= first) & (h - lag < end))
            def _():
                fn(h - lag)

        def at(step, fn):
            @pl.when(h == step)
            def _():
                fn()

        at(AT_SUM, early_sum)
        lagged(LAG_PREFIX, 0, normal, prefixes)
        causal(h)
        lagged(LAG_TOTAL, 0, normal, totals)
        at(AT_TOTAL, early_totals)
        at(AT_PREFIX, early_prefixes)
        lagged(LAG_FINISH, 0, normal, finish_normal)
        at(AT_SHARE, early_share)

        @pl.when(h == AT_FINISH)
        def _():
            wait_bytes(est.at[0], ed_recv)

            @pl.loop(normal, AT_FINISH)
            def _(g):
                finish_early(g)

        @pl.when(h > AT_FINISH)
        def _():
            finish_early(h - 1)

    finish_early(heads - 1)

    wait_bytes(ear.at[0], e_send)
    wait_bytes(precv.at[0 : ny - 1], p_send)
    wait_bytes(egat.at[0 : nz - 1], ea_send)
    wait_bytes(etot.at[0 : nx - 1], eb_send)
    wait_bytes(est.at[0, 0 : nz - 1], ec_send)
    wait_bytes(est.at[0], ed_send)

    @pl.loop(0, heads)
    def _(h):
        wait_bytes(xin.at[h, 0 : ny - 1], y_send.at[h])

    @pl.loop(0, normal)
    def _(h):
        wait_bytes(gat.at[h, 0 : row - 1], a_send.at[h])
        wait_bytes(tot.at[h, 0 : nx - 1], b_send.at[h])
        wait_bytes(st.at[h, 0 : row - 1], c_send.at[h])

    @pl.loop(0, early)
    def _(e):
        wait_bytes(mate.at[0, e], m_send.at[e])


def shards(nx, query, keys, values, grad_out):
    ny = lax.axis_size("head")
    nctx = lax.axis_size("ctx")
    row = nctx // nx
    nz = row // 2
    heads = query.shape[2] // ny // HD
    factor = (HD * BLOCK * nctx) ** (-0.5)
    per = 2 * HD // row
    early = min(EARLY, heads - 1)
    normal = heads - early
    dma = pltpu.SemaphoreType.DMA
    flops = heads * (9 * 2 * BLOCK * BLOCK * HD * 3 // 4 + 5 * 2 * BLOCK * HD * HD)
    ins = [pltpu.with_memory_space_constraint(a, pltpu.HBM) for a in (query, keys, values, grad_out)]
    f32, bf16 = jnp.float32, jnp.bfloat16
    return pl.pallas_call(
        functools.partial(kernel, heads, nx, row, factor),
        out_shape=[pltpu.VMEM((1, BLOCK, heads * HD), bf16)] * 3,
        in_specs=[pl.BlockSpec(memory_space=pltpu.HBM)] * 4,
        out_specs=[pl.BlockSpec(memory_space=pltpu.VMEM)] * 3,
        scratch_shapes=[
            pltpu.VMEM((heads, 4, BLOCK, HD), bf16),
            pltpu.VMEM((heads, 3, BLOCK, HD), f32),
            pltpu.VMEM((normal, 2 * HD, HD), f32),
            pltpu.VMEM((normal, row, per, HD), f32),
            pltpu.VMEM((normal, nx, per, HD), f32),
            pltpu.VMEM((normal, row, per, HD), bf16),
            pltpu.VMEM((normal, row, per, HD), bf16),
            pltpu.VMEM((2, ny, 2 * BLOCK // ny, early * HD), bf16),
            pltpu.VMEM((ny, early, HD, HD), bf16),
            pltpu.VMEM((ny, early, HD, HD), bf16),
            pltpu.VMEM((nz, early, per, HD), f32),
            pltpu.VMEM((nz, early, per, HD), f32),
            pltpu.VMEM((nx, early, per, HD), f32),
            pltpu.VMEM((nz, early, per, HD), f32),
            pltpu.VMEM((2, nz, early, per, HD), f32),
            pltpu.VMEM((2, early, HD, HD), f32),
            pltpu.SemaphoreType.REGULAR(((nz - 1).bit_length(),)),
        ]
        + [dma((heads,))] * 3
        + [dma((normal,))] * 6
        + [dma((early,))] * 2
        + [dma] * 13,
        compiler_params=pltpu.CompilerParams(
            collective_id=1, has_side_effects=True, vmem_limit_bytes=44 * 2**20
        ),
        cost_estimate=pl.CostEstimate(flops=flops, bytes_accessed=8 * 2**20, transcendentals=0),
    )(*ins)


def solution(mesh):
    nx = 4
    in_specs = (P("ctx", "head", None),) * 4
    out_specs = (P("ctx", None, "head"),) * 3
    return jax.shard_map(
        functools.partial(shards, nx), mesh=mesh, in_specs=in_specs, out_specs=out_specs, check_vma=False
    )
```

```python
import functools

import jax
import jax.numpy as jnp
from jax import lax
from jax.experimental import pallas as pl
from jax.experimental.pallas import tpu as pltpu
from jax.sharding import PartitionSpec as P

HD = 128
BLOCK = 512
HALF = 256
MESH = pl.DeviceIdType.MESH
NT = (((1,), (1,)), ((), ()))
NN = (((1,), (0,)), ((), ()))
TN = (((0,), (0,)), ((), ()))
WINDOW = 4
BEFORE = 1
AHEAD = 0
BUSY = 3
PIECES = 2
EARLY = 4
AT_SUM, AT_TOTAL, AT_PREFIX, AT_SHARE, AT_FINISH = 1, 2, 3, 5, 6
LAG_TOTAL, LAG_PREFIX, LAG_FINISH = 1, 2, 4


def dot(a, b, dims):
    return lax.dot_general(a, b, dims, preferred_element_type=jnp.float32)


def kernel(
    heads, nx, row, factor,
    q_in, k_in, v_in, g_in, gq_out, gk_out, gv_out,
    xin, acc, own, gat, tot, pre, st,
    ear, psend, precv, chip, egat, etot, epre, est, mate,
    rounds, y_send, y_recv, y_loc, a_send, a_recv, b_send, b_recv, c_send, c_recv,
    m_send, m_recv, e_loc, e_send, e_recv, p_send, p_recv,
    ea_send, ea_recv, eb_send, eb_recv, ec_send, ec_recv, ed_send, ed_recv,
):
    ny = lax.axis_size("head")
    y = lax.axis_index("head")
    ctx = lax.axis_index("ctx")
    nz = row // 2
    x = ctx // row
    me = ctx % row
    z = me // 2
    core = me % 2
    is_q = me // nz
    rows_y = BLOCK // ny
    ins = (q_in, k_in, v_in, g_in)
    per = 2 * HD // row
    early = ear.shape[3] // HD
    normal = heads - early
    dists = (2, 1, 3)

    row_order = sorted(range(1, row), key=lambda d: -min(d, row - d))
    z_order = sorted(range(1, nz), key=lambda d: -min(d, nz - d))
    x_order = sorted(range(1, nx), key=lambda d: -min(d, nx - d))

    def y_peer(d):
        return {"head": lax.rem(y + d, ny)}

    def place(x_at, z_at, core_at):
        return {"ctx": (x_at * nz + z_at) * 2 + core_at}

    def row_peer(d):
        t = lax.rem(me + d, row)
        return t, {"ctx": x * row + t}

    def x_peer(d):
        return {"ctx": lax.rem(x + d, nx) * row + me}

    partner = place(x, z, 1 - core)
    near = [y_peer(d) for d in dists] + [partner] + [x_peer(d) for d in (1, nx - 1)]

    def signal(sem, device):
        pl.semaphore_signal(sem, inc=1, device_id=device, device_id_type=MESH)

    def signal_line(sem, step):
        @pl.when(z >= step)
        def _():
            signal(sem, place(x, z - step, core))

        @pl.when(z + step < nz)
        def _():
            signal(sem, place(x, z + step, core))

    def line_count(step):
        return lax.min(z // step, 1) + lax.min((nz - 1 - z) // step, 1)

    barrier = pltpu.get_barrier_semaphore()
    for device in near:
        signal(barrier, device)
    signal_line(barrier, 1)
    pl.semaphore_wait(barrier, len(near) + line_count(1))

    def remote(src, dst, send, recv, device):
        pltpu.make_async_remote_copy(
            src_ref=src, dst_ref=dst, send_sem=send, recv_sem=recv,
            device_id=device, device_id_type=MESH,
        ).start()

    def wait_bytes(ref, sem):
        pltpu.make_async_copy(ref, ref, sem).wait()

    def my_rows(owner):
        return pl.ds(pl.multiple_of(owner * rows_y, rows_y), rows_y)

    def cols(owner, h, count=1):
        return pl.ds(pl.multiple_of((owner * heads + h) * HD, HD), count * HD)

    def send_y(h, arrays=range(4), local=True):
        for d in dists:
            tgt = lax.rem(y + d, ny)
            for a in arrays:
                remote(
                    ins[a].at[0, :, cols(tgt, h)], xin.at[h, a, my_rows(y), :],
                    y_send.at[h], y_recv.at[h], {"head": tgt},
                )
        for a in range(4 if local else 0):
            pltpu.make_async_copy(
                ins[a].at[0, :, cols(y, h)], xin.at[h, a, my_rows(y), :], y_loc.at[h]
            ).start()

    def early_rows():
        at = pl.ds(pl.multiple_of(core * rows_y, rows_y), rows_y)
        keys_side, query_side = (k_in, v_in), (q_in, g_in)

        def go(keep, give):
            for t in range(ny):
                for i in range(2):
                    src = (0, slice(None), cols(t, normal, early))
                    dst = ear.at[i, t, at, :]
                    remote(give[i].at[src], dst, e_send, e_recv, partner)
                    pltpu.make_async_copy(keep[i].at[src], dst, e_loc).start()

        @pl.when(core == 0)
        def _():
            go(keys_side, query_side)

        @pl.when(core == 1)
        def _():
            go(query_side, keys_side)

    def early_parts():
        wait_bytes(ear.at[0], e_loc)
        wait_bytes(ear.at[0], e_recv)
        for d in (2, 1, 3, 0):
            t = lax.rem(y + d, ny)
            for e in range(early):
                at = slice(e * HD, (e + 1) * HD)
                part = dot(ear[0, t, :, at], ear[1, t, :, at], TN)
                if d:
                    psend[d, e] = part.astype(jnp.bfloat16)
                else:
                    chip[:, e] = part.reshape(nz, per, HD)
            if d:
                remote(psend.at[d], precv.at[y], p_send, p_recv, y_peer(d))

    def early_sum():
        wait_bytes(precv.at[0 : ny - 1], p_recv)
        for e in range(early):
            total = chip[:, e]
            for d in range(1, ny):
                got = precv[lax.rem(y + d, ny), e].astype(jnp.float32)
                total = total + got.reshape(nz, per, HD)
            chip[:, e] = total
        for d in z_order:
            t = lax.rem(z + d, nz)
            remote(chip.at[t], egat.at[z], ea_send, ea_recv, place(x, t, core))
        egat[z] = chip[z]

    def early_totals():
        wait_bytes(egat.at[0 : nz - 1], ea_recv)
        total = egat[0]
        for s in range(1, nz):
            total = total + egat[s]
        etot[x] = total
        for d in x_order:
            remote(etot.at[x], etot.at[x], eb_send, eb_recv, x_peer(d))

    def base(parts, x_side):
        run = jnp.zeros(parts.shape[1:], jnp.float32)
        for s in range(nx):
            run = run + jnp.where((s - x) * x_side > 0, parts[s], 0.0)
        return run

    def early_prefixes():
        wait_bytes(etot.at[0 : nx - 1], eb_recv)
        run = base(etot, 2 * core - 1)
        for s in range(nz):
            at = s + core * (nz - 1 - 2 * s)
            epre[at] = run
            run = run + egat[at]
        for d in z_order:
            t = lax.rem(z + d, nz)
            remote(epre.at[t], est.at[core, z], ec_send, ec_recv, place(x, t, core))
        est[core, z] = epre[z]

    def early_share():
        wait_bytes(est.at[0, 0 : nz - 1], ec_recv)
        remote(est.at[core], est.at[core], ed_send, ed_recv, partner)

    def wait_y(h):
        wait_bytes(xin.at[h, 0 : ny - 1], y_recv.at[h])
        wait_bytes(xin.at[h, 0:1], y_loc.at[h])

    def states(h):
        own[h, 0:HD, :] = dot(xin[h, 1], xin[h, 2], TN)
        own[h, HD : 2 * HD, :] = dot(xin[h, 0], xin[h, 3], TN)
        for d in row_order:
            t, peer = row_peer(d)
            src = own.at[h, pl.ds(pl.multiple_of(t * per, per), per), :]
            remote(src, gat.at[h, me], a_send.at[h], a_recv.at[h], peer)
        gat[h, me] = own[h, pl.ds(pl.multiple_of(me * per, per), per), :]

    def late_state(h):
        e = h - normal
        mate[0, e] = dot(xin[h, 1 - core], xin[h, 2 + core], TN)
        remote(mate.at[0, e], mate.at[1, e], m_send.at[e], m_recv.at[e], partner)

    def totals(h):
        wait_bytes(gat.at[h, 0 : row - 1], a_recv.at[h])
        total = gat[h, 0]
        for s in range(1, row):
            total = total + gat[h, s]
        tot[h, x] = total
        for d in x_order:
            remote(tot.at[h, x], tot.at[h, x], b_send.at[h], b_recv.at[h], x_peer(d))

    def prefixes(h):
        wait_bytes(tot.at[h, 0 : nx - 1], b_recv.at[h])
        run = base(tot.at[h], 2 * is_q - 1)
        for s in range(row):
            at = s + is_q * (row - 1 - 2 * s)
            pre[h, at] = run.astype(jnp.bfloat16)
            run = run + gat[h, at]
        for d in row_order:
            t, peer = row_peer(d)
            remote(pre.at[h, t], st.at[h, me], c_send.at[h], c_recv.at[h], peer)
        st[h, me] = pre[h, me]

    r_at = lax.broadcasted_iota(jnp.int32, (HALF, HALF), 0)
    c_at = lax.broadcasted_iota(jnp.int32, (HALF, HALF), 1)

    def causal(h):
        lo, hi = pl.ds(0, HALF), pl.ds(HALF, HALF)

        def low(s):
            return jnp.where(r_at >= c_at, s, 0.0).astype(jnp.bfloat16)

        def upp(s):
            return jnp.where(r_at <= c_at, s, 0.0).astype(jnp.bfloat16)

        def part(a, at):
            return xin[h, a, at, :]

        def scores(left, right, first, other, last):
            s_first = dot(part(left, lo), part(right, lo), NT)
            s_last = dot(part(left, hi), part(right, hi), NT)
            s_other = dot(part(left, first), part(right, last), NT)
            return other(s_first), s_other.astype(jnp.bfloat16), other(s_last)

        a00, a10, a11 = scores(3, 2, hi, low, lo)
        acc[h, 0, lo, :] = dot(a00, part(1, lo), NN)
        acc[h, 0, hi, :] = dot(a10, part(1, lo), NN) + dot(a11, part(1, hi), NN)
        t00, t01, t11 = scores(2, 3, lo, upp, hi)
        acc[h, 1, lo, :] = dot(t00, part(0, lo), NN) + dot(t01, part(0, hi), NN)
        acc[h, 1, hi, :] = dot(t11, part(0, hi), NN)
        b00, b01, b11 = scores(1, 0, lo, upp, hi)
        acc[h, 2, lo, :] = dot(b00, part(3, lo), NN) + dot(b01, part(3, hi), NN)
        acc[h, 2, hi, :] = dot(b11, part(3, hi), NN)

    def finish(h, ks, qs):
        at = pl.ds(pl.multiple_of(h * HD, HD), HD)
        gq_out[0, :, at] = (factor * (acc[h, 0] + dot(xin[h, 3], ks, NT))).astype(jnp.bfloat16)
        gk_out[0, :, at] = (factor * (acc[h, 1] + dot(xin[h, 2], qs, NT))).astype(jnp.bfloat16)
        gv_out[0, :, at] = (factor * (acc[h, 2] + dot(xin[h, 1], qs, NN))).astype(jnp.bfloat16)

    def finish_normal(h):
        wait_bytes(st.at[h, 0 : row - 1], c_recv.at[h])
        ks = st[h, 0 : row // 2].reshape(HD, HD)
        qs = st[h, row // 2 : row].reshape(HD, HD)
        finish(h, ks, qs)

    def finish_early(h):
        e = h - normal
        wait_bytes(mate.at[0, e], m_recv.at[e])
        late = mate[1, e]
        ks = est[0, :, e].reshape(HD, HD) + jnp.where(core == 1, late, 0.0)
        qs = est[1, :, e].reshape(HD, HD) + jnp.where(core == 0, late, 0.0)
        finish(h, ks.astype(jnp.bfloat16), qs.astype(jnp.bfloat16))

    for h in range(min(WINDOW, BEFORE)):
        send_y(h)
    early_rows()
    if AHEAD:
        send_y(BEFORE, range(AHEAD), False)
    for r in range(rounds.shape[0]):
        signal_line(rounds.at[r], 2**r)
        if r == 0:
            for d in (1, nx - 1):
                signal(rounds.at[r], x_peer(d))
            early_parts()
            send_y(BEFORE, range(AHEAD, 4))
            for h in range(BEFORE + 1, min(WINDOW, heads)):
                send_y(h)
        pl.semaphore_wait(rounds.at[r], line_count(2**r) + (2 if r == 0 else 0))

    @pl.loop(0, heads)
    def _(h):
        @pl.when(h + WINDOW < heads)
        def _():
            send_y(h + WINDOW)

        wait_y(h)

        @pl.when(h < normal)
        def _():
            states(h)

        @pl.when(h >= normal)
        def _():
            late_state(h)

        def lagged(lag, first, end, fn):
            @pl.when((h - lag >= first) & (h - lag < end))
            def _():
                fn(h - lag)

        def at(step, fn):
            @pl.when(h == step)
            def _():
                fn()

        at(AT_SUM, early_sum)
        lagged(LAG_PREFIX, 0, normal, prefixes)
        lagged(LAG_TOTAL, BUSY, normal, totals)
        causal(h)
        lagged(LAG_TOTAL, 0, BUSY, totals)
        at(AT_TOTAL, early_totals)
        at(AT_PREFIX, early_prefixes)
        lagged(LAG_FINISH, 0, normal, finish_normal)
        at(AT_SHARE, early_share)

        @pl.when(h == AT_FINISH)
        def _():
            wait_bytes(est.at[0], ed_recv)

            @pl.loop(normal, AT_FINISH + 1)
            def _(g):
                finish_early(g)

        @pl.when(h > AT_FINISH)
        def _():
            finish_early(h)

    wait_bytes(ear.at[0], e_send)
    wait_bytes(precv.at[0 : ny - 1], p_send)
    wait_bytes(egat.at[0 : nz - 1], ea_send)
    wait_bytes(etot.at[0 : nx - 1], eb_send)
    wait_bytes(est.at[0, 0 : nz - 1], ec_send)
    wait_bytes(est.at[0], ed_send)

    @pl.loop(0, heads)
    def _(h):
        wait_bytes(xin.at[h, 0 : ny - 1], y_send.at[h])

    @pl.loop(0, normal)
    def _(h):
        wait_bytes(gat.at[h, 0 : row - 1], a_send.at[h])
        wait_bytes(tot.at[h, 0 : nx - 1], b_send.at[h])
        wait_bytes(st.at[h, 0 : row - 1], c_send.at[h])

    @pl.loop(0, early)
    def _(e):
        wait_bytes(mate.at[0, e], m_send.at[e])


def store(gq_in, gk_in, gv_in, gq_out, gk_out, gv_out, sems):
    pairs = ((gq_in, gq_out), (gk_in, gk_out), (gv_in, gv_out))
    copies = []
    for i, (src, dst) in enumerate(pairs):
        for j in range(sems.shape[1]):
            at = pl.ds(j * (BLOCK // sems.shape[1]), BLOCK // sems.shape[1])
            copies.append(pltpu.make_async_copy(src.at[0, at, :], dst.at[0, at, :], sems.at[i, j]))
    for copy in copies:
        copy.start()
    for copy in copies:
        copy.wait()


def shards(nx, query, keys, values, grad_out):
    ny = lax.axis_size("head")
    nctx = lax.axis_size("ctx")
    row = nctx // nx
    nz = row // 2
    heads = query.shape[2] // ny // HD
    factor = (HD * BLOCK * nctx) ** (-0.5)
    per = 2 * HD // row
    early = min(EARLY, heads - 1)
    normal = heads - early
    dma = pltpu.SemaphoreType.DMA
    flops = heads * (9 * 2 * BLOCK * BLOCK * HD * 3 // 4 + 5 * 2 * BLOCK * HD * HD)
    ins = [pltpu.with_memory_space_constraint(a, pltpu.HBM) for a in (query, keys, values, grad_out)]
    f32, bf16 = jnp.float32, jnp.bfloat16
    grads = pl.pallas_call(
        functools.partial(kernel, heads, nx, row, factor),
        out_shape=[pltpu.VMEM((1, BLOCK, heads * HD), bf16)] * 3,
        in_specs=[pl.BlockSpec(memory_space=pltpu.HBM)] * 4,
        out_specs=[pl.BlockSpec(memory_space=pltpu.VMEM)] * 3,
        scratch_shapes=[
            pltpu.VMEM((heads, 4, BLOCK, HD), bf16),
            pltpu.VMEM((heads, 3, BLOCK, HD), f32),
            pltpu.VMEM((normal, 2 * HD, HD), f32),
            pltpu.VMEM((normal, row, per, HD), f32),
            pltpu.VMEM((normal, nx, per, HD), f32),
            pltpu.VMEM((normal, row, per, HD), bf16),
            pltpu.VMEM((normal, row, per, HD), bf16),
            pltpu.VMEM((2, ny, 2 * BLOCK // ny, early * HD), bf16),
            pltpu.VMEM((ny, early, HD, HD), bf16),
            pltpu.VMEM((ny, early, HD, HD), bf16),
            pltpu.VMEM((nz, early, per, HD), f32),
            pltpu.VMEM((nz, early, per, HD), f32),
            pltpu.VMEM((nx, early, per, HD), f32),
            pltpu.VMEM((nz, early, per, HD), f32),
            pltpu.VMEM((2, nz, early, per, HD), f32),
            pltpu.VMEM((2, early, HD, HD), f32),
            pltpu.SemaphoreType.REGULAR(((nz - 1).bit_length(),)),
        ]
        + [dma((heads,))] * 3
        + [dma((normal,))] * 6
        + [dma((early,))] * 2
        + [dma] * 13,
        compiler_params=pltpu.CompilerParams(
            collective_id=1, has_side_effects=True, vmem_limit_bytes=44 * 2**20
        ),
        cost_estimate=pl.CostEstimate(flops=flops, bytes_accessed=8 * 2**20, transcendentals=0),
    )(*ins)
    return pl.pallas_call(
        store,
        out_shape=[jax.ShapeDtypeStruct(a.shape, a.dtype) for a in grads],
        in_specs=[pl.BlockSpec(memory_space=pltpu.VMEM)] * 3,
        out_specs=[pl.BlockSpec(memory_space=pltpu.HBM)] * 3,
        scratch_shapes=[dma((3, PIECES))],
    )(*[pltpu.with_memory_space_constraint(a, pltpu.VMEM) for a in grads])


def solution(mesh):
    nx = 4
    in_specs = (P("ctx", "head", None),) * 4
    out_specs = (P("ctx", None, "head"),) * 3
    return jax.shard_map(
        functools.partial(shards, nx), mesh=mesh, in_specs=in_specs, out_specs=out_specs, check_vma=False
    )
```

```python
import functools

import jax
import jax.numpy as jnp
from jax import lax
from jax.experimental import pallas as pl
from jax.experimental.pallas import tpu as pltpu
from jax.sharding import PartitionSpec as P

HD = 128
BLOCK = 512
HALF = 256
MESH = pl.DeviceIdType.MESH
NT = (((1,), (1,)), ((), ()))
NN = (((1,), (0,)), ((), ()))
TN = (((0,), (0,)), ((), ()))
WINDOW = 5
BEFORE = 1
BETWEEN = 2
BUSY = 3
PIECES = 2
EARLY = 4
AT_SUM, AT_TOTAL, AT_PREFIX, AT_SHARE, AT_FINISH = 1, 2, 3, 5, 6
LAG_TOTAL, LAG_PREFIX, LAG_FINISH = 1, 2, 4


def dot(a, b, dims):
    return lax.dot_general(a, b, dims, preferred_element_type=jnp.float32)


def kernel(
    heads, nx, row, factor,
    q_in, k_in, v_in, g_in, gq_out, gk_out, gv_out,
    xin, acc, own, gat, tot, pre, st,
    ear, psend, pkeep, phop, precv, chip, egat, etot, epre, est, mate,
    rounds, y_send, y_recv, y_loc, a_send, a_recv, b_send, b_recv, c_send, c_recv,
    m_send, m_recv, e_loc, e_send, e_recv, h_send, h_recv, p_send, p_recv,
    ea_send, ea_recv, eb_send, eb_recv, ec_send, ec_recv, ed_send, ed_recv,
):
    ny = lax.axis_size("head")
    y = lax.axis_index("head")
    ctx = lax.axis_index("ctx")
    nz = row // 2
    x = ctx // row
    me = ctx % row
    z = me // 2
    core = me % 2
    is_q = me // nz
    rows_y = BLOCK // ny
    ins = (q_in, k_in, v_in, g_in)
    per = 2 * HD // row
    early = ear.shape[3] // HD
    normal = heads - early
    dists = (2, 1, 3)

    row_order = sorted(range(1, row), key=lambda d: -min(d, row - d))
    z_order = sorted(range(1, nz), key=lambda d: -min(d, nz - d))
    x_order = sorted(range(1, nx), key=lambda d: -min(d, nx - d))

    def y_peer(d):
        return {"head": lax.rem(y + d, ny)}

    def place(x_at, z_at, core_at):
        return {"ctx": (x_at * nz + z_at) * 2 + core_at}

    def row_peer(d):
        t = lax.rem(me + d, row)
        return t, {"ctx": x * row + t}

    def x_peer(d):
        return {"ctx": lax.rem(x + d, nx) * row + me}

    partner = place(x, z, 1 - core)
    near = [y_peer(d) for d in dists] + [partner] + [x_peer(d) for d in (1, nx - 1)]

    def signal(sem, device):
        pl.semaphore_signal(sem, inc=1, device_id=device, device_id_type=MESH)

    def signal_line(sem, step):
        @pl.when(z >= step)
        def _():
            signal(sem, place(x, z - step, core))

        @pl.when(z + step < nz)
        def _():
            signal(sem, place(x, z + step, core))

    def line_count(step):
        return lax.min(z // step, 1) + lax.min((nz - 1 - z) // step, 1)

    barrier = pltpu.get_barrier_semaphore()
    for device in near:
        signal(barrier, device)
    signal_line(barrier, 1)
    pl.semaphore_wait(barrier, len(near) + line_count(1))

    def remote(src, dst, send, recv, device):
        pltpu.make_async_remote_copy(
            src_ref=src, dst_ref=dst, send_sem=send, recv_sem=recv,
            device_id=device, device_id_type=MESH,
        ).start()

    def wait_bytes(ref, sem):
        pltpu.make_async_copy(ref, ref, sem).wait()

    def my_rows(owner):
        return pl.ds(pl.multiple_of(owner * rows_y, rows_y), rows_y)

    def cols(owner, h, count=1):
        return pl.ds(pl.multiple_of((owner * heads + h) * HD, HD), count * HD)

    def send_y(h):
        for d in dists:
            tgt = lax.rem(y + d, ny)
            for a in range(4):
                remote(
                    ins[a].at[0, :, cols(tgt, h)], xin.at[h, a, my_rows(y), :],
                    y_send.at[h], y_recv.at[h], {"head": tgt},
                )
        for a in range(4):
            pltpu.make_async_copy(
                ins[a].at[0, :, cols(y, h)], xin.at[h, a, my_rows(y), :], y_loc.at[h]
            ).start()

    def early_rows():
        at = pl.ds(pl.multiple_of(core * rows_y, rows_y), rows_y)
        keys_side, query_side = (k_in, v_in), (q_in, g_in)

        def go(keep, give):
            for t in range(ny):
                for i in range(2):
                    src = (0, slice(None), cols(t, normal, early))
                    dst = ear.at[i, t, at, :]
                    remote(give[i].at[src], dst, e_send, e_recv, partner)
                    pltpu.make_async_copy(keep[i].at[src], dst, e_loc).start()

        @pl.when(core == 0)
        def _():
            go(keys_side, query_side)

        @pl.when(core == 1)
        def _():
            go(query_side, keys_side)

    def early_parts():
        wait_bytes(ear.at[0], e_loc)
        wait_bytes(ear.at[0], e_recv)
        top, low = slice(0, HD // 2), slice(HD // 2, HD)
        for d in (2, 1, 3, 0):
            t = lax.rem(y + d, ny)
            for e in range(early):
                at = slice(e * HD, (e + 1) * HD)
                part = dot(ear[0, t, :, at], ear[1, t, :, at], TN)
                if d == 0:
                    chip[:, e] = part.reshape(nz, per, HD)
                elif d == 2:
                    psend[0, e] = part[top].astype(jnp.bfloat16)
                    psend[1, e] = part[low].astype(jnp.bfloat16)
                elif d == 1:
                    psend[2, e] = part[top].astype(jnp.bfloat16)
                    pkeep[0, e] = part[low]
                else:
                    psend[3, e] = part[low].astype(jnp.bfloat16)
                    pkeep[1, e] = part[top]
            if d == 2:
                remote(psend.at[0], phop.at[0], h_send, h_recv, y_peer(ny - 1))
                remote(psend.at[1], phop.at[1], h_send, h_recv, y_peer(1))
            elif d == 1:
                remote(psend.at[2], precv.at[0, 0], p_send, p_recv, y_peer(1))
            elif d == 3:
                remote(psend.at[3], precv.at[1, 1], p_send, p_recv, y_peer(ny - 1))

    def early_merge():
        wait_bytes(phop, h_recv)
        for e in range(early):
            psend[4, e] = (pkeep[0, e] + phop[1, e].astype(jnp.float32)).astype(jnp.bfloat16)
            psend[5, e] = (pkeep[1, e] + phop[0, e].astype(jnp.float32)).astype(jnp.bfloat16)
        remote(psend.at[4], precv.at[0, 1], p_send, p_recv, y_peer(1))
        remote(psend.at[5], precv.at[1, 0], p_send, p_recv, y_peer(ny - 1))

    def early_sum():
        wait_bytes(precv, p_recv)
        half = nz // 2
        for e in range(early):
            for i in range(2):
                at = slice(i * half, (i + 1) * half)
                got = precv[0, i, e].astype(jnp.float32) + precv[1, i, e].astype(jnp.float32)
                chip[at, e] = chip[at, e] + got.reshape(half, per, HD)
        for d in z_order:
            t = lax.rem(z + d, nz)
            remote(chip.at[t], egat.at[z], ea_send, ea_recv, place(x, t, core))
        egat[z] = chip[z]

    def early_totals():
        wait_bytes(egat.at[0 : nz - 1], ea_recv)
        total = egat[0]
        for s in range(1, nz):
            total = total + egat[s]
        etot[x] = total
        for d in x_order:
            remote(etot.at[x], etot.at[x], eb_send, eb_recv, x_peer(d))

    def base(parts, x_side):
        run = jnp.zeros(parts.shape[1:], jnp.float32)
        for s in range(nx):
            run = run + jnp.where((s - x) * x_side > 0, parts[s], 0.0)
        return run

    def early_prefixes():
        wait_bytes(etot.at[0 : nx - 1], eb_recv)
        run = base(etot, 2 * core - 1)
        for s in range(nz):
            at = s + core * (nz - 1 - 2 * s)
            epre[at] = run
            run = run + egat[at]
        for d in z_order:
            t = lax.rem(z + d, nz)
            remote(epre.at[t], est.at[core, z], ec_send, ec_recv, place(x, t, core))
        est[core, z] = epre[z]

    def early_share():
        wait_bytes(est.at[0, 0 : nz - 1], ec_recv)
        remote(est.at[core], est.at[core], ed_send, ed_recv, partner)

    def wait_y(h):
        wait_bytes(xin.at[h, 0 : ny - 1], y_recv.at[h])
        wait_bytes(xin.at[h, 0:1], y_loc.at[h])

    def states(h):
        own[h, 0:HD, :] = dot(xin[h, 1], xin[h, 2], TN)
        own[h, HD : 2 * HD, :] = dot(xin[h, 0], xin[h, 3], TN)
        for d in row_order:
            t, peer = row_peer(d)
            src = own.at[h, pl.ds(pl.multiple_of(t * per, per), per), :]
            remote(src, gat.at[h, me], a_send.at[h], a_recv.at[h], peer)
        gat[h, me] = own[h, pl.ds(pl.multiple_of(me * per, per), per), :]

    def late_state(h):
        e = h - normal
        mate[0, e] = dot(xin[h, 1 - core], xin[h, 2 + core], TN)
        remote(mate.at[0, e], mate.at[1, e], m_send.at[e], m_recv.at[e], partner)

    def totals(h):
        wait_bytes(gat.at[h, 0 : row - 1], a_recv.at[h])
        total = gat[h, 0]
        for s in range(1, row):
            total = total + gat[h, s]
        tot[h, x] = total
        for d in x_order:
            remote(tot.at[h, x], tot.at[h, x], b_send.at[h], b_recv.at[h], x_peer(d))

    def prefixes(h):
        wait_bytes(tot.at[h, 0 : nx - 1], b_recv.at[h])
        run = base(tot.at[h], 2 * is_q - 1)
        for s in range(row):
            at = s + is_q * (row - 1 - 2 * s)
            pre[h, at] = run.astype(jnp.bfloat16)
            run = run + gat[h, at]
        for d in row_order:
            t, peer = row_peer(d)
            remote(pre.at[h, t], st.at[h, me], c_send.at[h], c_recv.at[h], peer)
        st[h, me] = pre[h, me]

    r_at = lax.broadcasted_iota(jnp.int32, (HALF, HALF), 0)
    c_at = lax.broadcasted_iota(jnp.int32, (HALF, HALF), 1)

    def causal(h):
        lo, hi = pl.ds(0, HALF), pl.ds(HALF, HALF)

        def low(s):
            return jnp.where(r_at >= c_at, s, 0.0).astype(jnp.bfloat16)

        def upp(s):
            return jnp.where(r_at <= c_at, s, 0.0).astype(jnp.bfloat16)

        def part(a, at):
            return xin[h, a, at, :]

        def scores(left, right, first, other, last):
            s_first = dot(part(left, lo), part(right, lo), NT)
            s_last = dot(part(left, hi), part(right, hi), NT)
            s_other = dot(part(left, first), part(right, last), NT)
            return other(s_first), s_other.astype(jnp.bfloat16), other(s_last)

        a00, a10, a11 = scores(3, 2, hi, low, lo)
        acc[h, 0, lo, :] = dot(a00, part(1, lo), NN)
        acc[h, 0, hi, :] = dot(a10, part(1, lo), NN) + dot(a11, part(1, hi), NN)
        t00, t01, t11 = scores(2, 3, lo, upp, hi)
        acc[h, 1, lo, :] = dot(t00, part(0, lo), NN) + dot(t01, part(0, hi), NN)
        acc[h, 1, hi, :] = dot(t11, part(0, hi), NN)
        b00, b01, b11 = scores(1, 0, lo, upp, hi)
        acc[h, 2, lo, :] = dot(b00, part(3, lo), NN) + dot(b01, part(3, hi), NN)
        acc[h, 2, hi, :] = dot(b11, part(3, hi), NN)

    def finish(h, ks, qs):
        at = pl.ds(pl.multiple_of(h * HD, HD), HD)
        gq_out[0, :, at] = (factor * (acc[h, 0] + dot(xin[h, 3], ks, NT))).astype(jnp.bfloat16)
        gk_out[0, :, at] = (factor * (acc[h, 1] + dot(xin[h, 2], qs, NT))).astype(jnp.bfloat16)
        gv_out[0, :, at] = (factor * (acc[h, 2] + dot(xin[h, 1], qs, NN))).astype(jnp.bfloat16)

    def finish_normal(h):
        wait_bytes(st.at[h, 0 : row - 1], c_recv.at[h])
        ks = st[h, 0 : row // 2].reshape(HD, HD)
        qs = st[h, row // 2 : row].reshape(HD, HD)
        finish(h, ks, qs)

    def finish_early(h):
        e = h - normal
        wait_bytes(mate.at[0, e], m_recv.at[e])
        late = mate[1, e]
        ks = est[0, :, e].reshape(HD, HD) + jnp.where(core == 1, late, 0.0)
        qs = est[1, :, e].reshape(HD, HD) + jnp.where(core == 0, late, 0.0)
        finish(h, ks.astype(jnp.bfloat16), qs.astype(jnp.bfloat16))

    def wait_round(r):
        pl.semaphore_wait(rounds.at[r], line_count(2**r) + (2 if r == 0 else 0))

    for h in range(BEFORE):
        send_y(h)
    early_rows()
    signal_line(rounds.at[0], 1)
    for d in (1, nx - 1):
        signal(rounds.at[0], x_peer(d))
    early_parts()
    for h in range(BEFORE, BETWEEN):
        send_y(h)
    wait_round(0)
    signal_line(rounds.at[1], 2)
    early_merge()
    for h in range(BETWEEN, min(WINDOW, heads)):
        send_y(h)
    for r in range(1, rounds.shape[0]):
        wait_round(r)
        if r + 1 < rounds.shape[0]:
            signal_line(rounds.at[r + 1], 2 ** (r + 1))

    @pl.loop(0, heads)
    def _(h):
        @pl.when(h + WINDOW < heads)
        def _():
            send_y(h + WINDOW)

        wait_y(h)

        @pl.when(h < normal)
        def _():
            states(h)

        @pl.when(h >= normal)
        def _():
            late_state(h)

        def lagged(lag, first, end, fn):
            @pl.when((h - lag >= first) & (h - lag < end))
            def _():
                fn(h - lag)

        def at(step, fn):
            @pl.when(h == step)
            def _():
                fn()

        at(AT_SUM, early_sum)
        lagged(LAG_PREFIX, 0, normal, prefixes)
        lagged(LAG_TOTAL, BUSY, normal, totals)
        causal(h)
        lagged(LAG_TOTAL, 0, BUSY, totals)
        at(AT_TOTAL, early_totals)
        at(AT_PREFIX, early_prefixes)
        lagged(LAG_FINISH, 0, normal, finish_normal)
        at(AT_SHARE, early_share)

        @pl.when(h == AT_FINISH)
        def _():
            wait_bytes(est.at[0], ed_recv)

            @pl.loop(normal, AT_FINISH + 1)
            def _(g):
                finish_early(g)

        @pl.when(h > AT_FINISH)
        def _():
            finish_early(h)

    wait_bytes(ear.at[0], e_send)
    wait_bytes(phop, h_send)
    wait_bytes(precv, p_send)
    wait_bytes(egat.at[0 : nz - 1], ea_send)
    wait_bytes(etot.at[0 : nx - 1], eb_send)
    wait_bytes(est.at[0, 0 : nz - 1], ec_send)
    wait_bytes(est.at[0], ed_send)

    @pl.loop(0, heads)
    def _(h):
        wait_bytes(xin.at[h, 0 : ny - 1], y_send.at[h])

    @pl.loop(0, normal)
    def _(h):
        wait_bytes(gat.at[h, 0 : row - 1], a_send.at[h])
        wait_bytes(tot.at[h, 0 : nx - 1], b_send.at[h])
        wait_bytes(st.at[h, 0 : row - 1], c_send.at[h])

    @pl.loop(0, early)
    def _(e):
        wait_bytes(mate.at[0, e], m_send.at[e])


def store(gq_in, gk_in, gv_in, gq_out, gk_out, gv_out, sems):
    pairs = ((gq_in, gq_out), (gk_in, gk_out), (gv_in, gv_out))
    copies = []
    for i, (src, dst) in enumerate(pairs):
        for j in range(sems.shape[1]):
            at = pl.ds(j * (BLOCK // sems.shape[1]), BLOCK // sems.shape[1])
            copies.append(pltpu.make_async_copy(src.at[0, at, :], dst.at[0, at, :], sems.at[i, j]))
    for copy in copies:
        copy.start()
    for copy in copies:
        copy.wait()


def shards(nx, query, keys, values, grad_out):
    ny = lax.axis_size("head")
    nctx = lax.axis_size("ctx")
    row = nctx // nx
    nz = row // 2
    heads = query.shape[2] // ny // HD
    factor = (HD * BLOCK * nctx) ** (-0.5)
    per = 2 * HD // row
    early = min(EARLY, heads - 1)
    normal = heads - early
    dma = pltpu.SemaphoreType.DMA
    flops = heads * (9 * 2 * BLOCK * BLOCK * HD * 3 // 4 + 5 * 2 * BLOCK * HD * HD)
    ins = [pltpu.with_memory_space_constraint(a, pltpu.HBM) for a in (query, keys, values, grad_out)]
    f32, bf16 = jnp.float32, jnp.bfloat16
    grads = pl.pallas_call(
        functools.partial(kernel, heads, nx, row, factor),
        out_shape=[pltpu.VMEM((1, BLOCK, heads * HD), bf16)] * 3,
        in_specs=[pl.BlockSpec(memory_space=pltpu.HBM)] * 4,
        out_specs=[pl.BlockSpec(memory_space=pltpu.VMEM)] * 3,
        scratch_shapes=[
            pltpu.VMEM((heads, 4, BLOCK, HD), bf16),
            pltpu.VMEM((heads, 3, BLOCK, HD), f32),
            pltpu.VMEM((normal, 2 * HD, HD), f32),
            pltpu.VMEM((normal, row, per, HD), f32),
            pltpu.VMEM((normal, nx, per, HD), f32),
            pltpu.VMEM((normal, row, per, HD), bf16),
            pltpu.VMEM((normal, row, per, HD), bf16),
            pltpu.VMEM((2, ny, 2 * BLOCK // ny, early * HD), bf16),
            pltpu.VMEM((6, early, HD // 2, HD), bf16),
            pltpu.VMEM((2, early, HD // 2, HD), f32),
            pltpu.VMEM((2, early, HD // 2, HD), bf16),
            pltpu.VMEM((2, 2, early, HD // 2, HD), bf16),
            pltpu.VMEM((nz, early, per, HD), f32),
            pltpu.VMEM((nz, early, per, HD), f32),
            pltpu.VMEM((nx, early, per, HD), f32),
            pltpu.VMEM((nz, early, per, HD), f32),
            pltpu.VMEM((2, nz, early, per, HD), f32),
            pltpu.VMEM((2, early, HD, HD), f32),
            pltpu.SemaphoreType.REGULAR(((nz - 1).bit_length(),)),
        ]
        + [dma((heads,))] * 3
        + [dma((normal,))] * 6
        + [dma((early,))] * 2
        + [dma] * 15,
        compiler_params=pltpu.CompilerParams(
            collective_id=1, has_side_effects=True, vmem_limit_bytes=44 * 2**20
        ),
        cost_estimate=pl.CostEstimate(flops=flops, bytes_accessed=8 * 2**20, transcendentals=0),
    )(*ins)
    return pl.pallas_call(
        store,
        out_shape=[jax.ShapeDtypeStruct(a.shape, a.dtype) for a in grads],
        in_specs=[pl.BlockSpec(memory_space=pltpu.VMEM)] * 3,
        out_specs=[pl.BlockSpec(memory_space=pltpu.HBM)] * 3,
        scratch_shapes=[dma((3, PIECES))],
    )(*[pltpu.with_memory_space_constraint(a, pltpu.VMEM) for a in grads])


def solution(mesh):
    nx = 4
    in_specs = (P("ctx", "head", None),) * 4
    out_specs = (P("ctx", None, "head"),) * 3
    return jax.shard_map(
        functools.partial(shards, nx), mesh=mesh, in_specs=in_specs, out_specs=out_specs, check_vma=False
    )
```

```python
import functools

import jax
import jax.numpy as jnp
from jax import lax
from jax.experimental import pallas as pl
from jax.experimental.pallas import tpu as pltpu
from jax.sharding import PartitionSpec as P

HD = 128
BLOCK = 512
HALF = 256
MESH = pl.DeviceIdType.MESH
NT = (((1,), (1,)), ((), ()))
NN = (((1,), (0,)), ((), ()))
TN = (((0,), (0,)), ((), ()))
WINDOW = 6
BEFORE = 1
BETWEEN = 2
BUSY = 3
PIECES = 2
EARLY = 4
AT_SUM, AT_TOTAL, AT_PREFIX, AT_SHARE, AT_FINISH = 1, 2, 3, 5, 6
LAG_TOTAL, LAG_PREFIX, LAG_FINISH = 1, 2, 4


def dot(a, b, dims):
    return lax.dot_general(a, b, dims, preferred_element_type=jnp.float32)


def kernel(
    heads, nx, row, factor,
    q_in, k_in, v_in, g_in, gq_out, gk_out, gv_out,
    xin, acc, own, gat, tot, pre, st,
    ear, psend, pkeep, phop, precv, chip, egat, etot, epre, est, mate,
    rounds, reply, y_send, y_recv, y_loc, a_send, a_recv, b_send, b_recv, c_send, c_recv,
    m_send, m_recv, e_loc, e_send, e_recv, h_send, h_recv, p_send, p_recv,
    ea_send, ea_recv, eb_send, eb_recv, ec_send, ec_recv, ed_send, ed_recv,
):
    ny = lax.axis_size("head")
    y = lax.axis_index("head")
    ctx = lax.axis_index("ctx")
    nz = row // 2
    x = ctx // row
    me = ctx % row
    z = me // 2
    core = me % 2
    is_q = me // nz
    rows_y = BLOCK // ny
    ins = (q_in, k_in, v_in, g_in)
    per = 2 * HD // row
    early = ear.shape[3] // HD
    normal = heads - early
    dists = (2, 1, 3)

    row_order = sorted(range(1, row), key=lambda d: -min(d, row - d))
    z_order = sorted(range(1, nz), key=lambda d: -min(d, nz - d))
    x_order = sorted(range(1, nx), key=lambda d: -min(d, nx - d))

    def y_peer(d):
        return {"head": lax.rem(y + d, ny)}

    def place(x_at, z_at, core_at):
        return {"ctx": (x_at * nz + z_at) * 2 + core_at}

    def row_peer(d):
        t = lax.rem(me + d, row)
        return t, {"ctx": x * row + t}

    def x_peer(d):
        return {"ctx": lax.rem(x + d, nx) * row + me}

    partner = place(x, z, 1 - core)

    def signal(sem, device):
        pl.semaphore_signal(sem, inc=1, device_id=device, device_id_type=MESH)

    def signal_line(sem, step):
        @pl.when(z >= step)
        def _():
            signal(sem, place(x, z - step, core))

        @pl.when(z + step < nz)
        def _():
            signal(sem, place(x, z + step, core))

        if step < nx:
            @pl.when(x >= step)
            def _():
                signal(sem, place(x - step, z, core))

            @pl.when(x + step < nx)
            def _():
                signal(sem, place(x + step, z, core))

    def line_count(step):
        count = lax.min(z // step, 1) + lax.min((nz - 1 - z) // step, 1)
        return count + lax.min(x // step, 1) + lax.min((nx - 1 - x) // step, 1)

    barrier = pltpu.get_barrier_semaphore()
    for d in dists:
        signal(barrier, y_peer(d))

    @pl.when(core == 1)
    def _():
        signal(barrier, partner)

    @pl.when(z + 1 < nz)
    def _():
        signal(barrier, place(x, z + 1, core))

    @pl.when(x + 1 < nx)
    def _():
        signal(barrier, place(x + 1, z, core))

    pl.semaphore_wait(barrier, ny - 1 + (1 - core) + lax.min(z, 1) + lax.min(x, 1))

    @pl.when(core == 0)
    def _():
        signal(reply.at[0], partner)

    @pl.when(z >= 1)
    def _():
        signal(reply.at[1], place(x, z - 1, core))

    @pl.when(x >= 1)
    def _():
        signal(reply.at[2], place(x - 1, z, core))

    def remote(src, dst, send, recv, device):
        pltpu.make_async_remote_copy(
            src_ref=src, dst_ref=dst, send_sem=send, recv_sem=recv,
            device_id=device, device_id_type=MESH,
        ).start()

    def wait_bytes(ref, sem):
        pltpu.make_async_copy(ref, ref, sem).wait()

    def my_rows(owner):
        return pl.ds(pl.multiple_of(owner * rows_y, rows_y), rows_y)

    def cols(owner, h, count=1):
        return pl.ds(pl.multiple_of((owner * heads + h) * HD, HD), count * HD)

    def send_y(h):
        for d in dists:
            tgt = lax.rem(y + d, ny)
            for a in range(4):
                remote(
                    ins[a].at[0, :, cols(tgt, h)], xin.at[h, a, my_rows(y), :],
                    y_send.at[h], y_recv.at[h], {"head": tgt},
                )
        for a in range(4):
            pltpu.make_async_copy(
                ins[a].at[0, :, cols(y, h)], xin.at[h, a, my_rows(y), :], y_loc.at[h]
            ).start()

    def early_rows():
        at = pl.ds(pl.multiple_of(core * rows_y, rows_y), rows_y)
        keys_side, query_side = (k_in, v_in), (q_in, g_in)

        def go(keep, give):
            for t in range(ny):
                for i in range(2):
                    src = (0, slice(None), cols(t, normal, early))
                    dst = ear.at[i, t, at, :]
                    remote(give[i].at[src], dst, e_send, e_recv, partner)
                    pltpu.make_async_copy(keep[i].at[src], dst, e_loc).start()

        @pl.when(core == 0)
        def _():
            go(keys_side, query_side)

        @pl.when(core == 1)
        def _():
            go(query_side, keys_side)

    def early_parts():
        wait_bytes(ear.at[0], e_loc)
        wait_bytes(ear.at[0], e_recv)
        top, low = slice(0, HD // 2), slice(HD // 2, HD)
        for d in (2, 1, 3, 0):
            t = lax.rem(y + d, ny)
            for e in range(early):
                at = slice(e * HD, (e + 1) * HD)
                part = dot(ear[0, t, :, at], ear[1, t, :, at], TN)
                if d == 0:
                    chip[:, e] = part.reshape(nz, per, HD)
                elif d == 2:
                    psend[0, e] = part[top].astype(jnp.bfloat16)
                    psend[1, e] = part[low].astype(jnp.bfloat16)
                elif d == 1:
                    psend[2, e] = part[top].astype(jnp.bfloat16)
                    pkeep[0, e] = part[low]
                else:
                    psend[3, e] = part[low].astype(jnp.bfloat16)
                    pkeep[1, e] = part[top]
            if d == 2:
                remote(psend.at[0], phop.at[0], h_send, h_recv, y_peer(ny - 1))
                remote(psend.at[1], phop.at[1], h_send, h_recv, y_peer(1))
            elif d == 1:
                remote(psend.at[2], precv.at[0, 0], p_send, p_recv, y_peer(1))
            elif d == 3:
                remote(psend.at[3], precv.at[1, 1], p_send, p_recv, y_peer(ny - 1))

    def early_merge():
        wait_bytes(phop, h_recv)
        for e in range(early):
            psend[4, e] = (pkeep[0, e] + phop[1, e].astype(jnp.float32)).astype(jnp.bfloat16)
            psend[5, e] = (pkeep[1, e] + phop[0, e].astype(jnp.float32)).astype(jnp.bfloat16)
        remote(psend.at[4], precv.at[0, 1], p_send, p_recv, y_peer(1))
        remote(psend.at[5], precv.at[1, 0], p_send, p_recv, y_peer(ny - 1))

    def early_sum():
        wait_bytes(precv, p_recv)
        half = nz // 2
        for e in range(early):
            for i in range(2):
                at = slice(i * half, (i + 1) * half)
                got = precv[0, i, e].astype(jnp.float32) + precv[1, i, e].astype(jnp.float32)
                chip[at, e] = chip[at, e] + got.reshape(half, per, HD)
        for d in z_order:
            t = lax.rem(z + d, nz)
            remote(chip.at[t], egat.at[z], ea_send, ea_recv, place(x, t, core))
        egat[z] = chip[z]

    def early_totals():
        wait_bytes(egat.at[0 : nz - 1], ea_recv)
        total = egat[0]
        for s in range(1, nz):
            total = total + egat[s]
        etot[x] = total
        for d in x_order:
            remote(etot.at[x], etot.at[x], eb_send, eb_recv, x_peer(d))

    def base(parts, x_side):
        run = jnp.zeros(parts.shape[1:], jnp.float32)
        for s in range(nx):
            run = run + jnp.where((s - x) * x_side > 0, parts[s], 0.0)
        return run

    def early_prefixes():
        wait_bytes(etot.at[0 : nx - 1], eb_recv)
        run = base(etot, 2 * core - 1)
        for s in range(nz):
            at = s + core * (nz - 1 - 2 * s)
            epre[at] = run
            run = run + egat[at]
        for d in z_order:
            t = lax.rem(z + d, nz)
            remote(epre.at[t], est.at[core, z], ec_send, ec_recv, place(x, t, core))
        est[core, z] = epre[z]

    def early_share():
        wait_bytes(est.at[0, 0 : nz - 1], ec_recv)
        remote(est.at[core], est.at[core], ed_send, ed_recv, partner)

    def wait_y(h):
        wait_bytes(xin.at[h, 0 : ny - 1], y_recv.at[h])
        wait_bytes(xin.at[h, 0:1], y_loc.at[h])

    def states(h):
        own[h, 0:HD, :] = dot(xin[h, 1], xin[h, 2], TN)
        own[h, HD : 2 * HD, :] = dot(xin[h, 0], xin[h, 3], TN)
        for d in row_order:
            t, peer = row_peer(d)
            src = own.at[h, pl.ds(pl.multiple_of(t * per, per), per), :]
            remote(src, gat.at[h, me], a_send.at[h], a_recv.at[h], peer)
        gat[h, me] = own[h, pl.ds(pl.multiple_of(me * per, per), per), :]

    def late_state(h):
        e = h - normal
        mate[0, e] = dot(xin[h, 1 - core], xin[h, 2 + core], TN)
        remote(mate.at[0, e], mate.at[1, e], m_send.at[e], m_recv.at[e], partner)

    def totals(h):
        wait_bytes(gat.at[h, 0 : row - 1], a_recv.at[h])
        total = gat[h, 0]
        for s in range(1, row):
            total = total + gat[h, s]
        tot[h, x] = total
        for d in x_order:
            remote(tot.at[h, x], tot.at[h, x], b_send.at[h], b_recv.at[h], x_peer(d))

    def prefixes(h):
        wait_bytes(tot.at[h, 0 : nx - 1], b_recv.at[h])
        run = base(tot.at[h], 2 * is_q - 1)
        for s in range(row):
            at = s + is_q * (row - 1 - 2 * s)
            pre[h, at] = run.astype(jnp.bfloat16)
            run = run + gat[h, at]
        for d in row_order:
            t, peer = row_peer(d)
            remote(pre.at[h, t], st.at[h, me], c_send.at[h], c_recv.at[h], peer)
        st[h, me] = pre[h, me]

    r_at = lax.broadcasted_iota(jnp.int32, (HALF, HALF), 0)
    c_at = lax.broadcasted_iota(jnp.int32, (HALF, HALF), 1)

    def causal(h):
        lo, hi = pl.ds(0, HALF), pl.ds(HALF, HALF)

        def low(s):
            return jnp.where(r_at >= c_at, s, 0.0).astype(jnp.bfloat16)

        def upp(s):
            return jnp.where(r_at <= c_at, s, 0.0).astype(jnp.bfloat16)

        def part(a, at):
            return xin[h, a, at, :]

        def scores(left, right, first, other, last):
            s_first = dot(part(left, lo), part(right, lo), NT)
            s_last = dot(part(left, hi), part(right, hi), NT)
            s_other = dot(part(left, first), part(right, last), NT)
            return other(s_first), s_other.astype(jnp.bfloat16), other(s_last)

        a00, a10, a11 = scores(3, 2, hi, low, lo)
        acc[h, 0, lo, :] = dot(a00, part(1, lo), NN)
        acc[h, 0, hi, :] = dot(a10, part(1, lo), NN) + dot(a11, part(1, hi), NN)
        t00, t01, t11 = scores(2, 3, lo, upp, hi)
        acc[h, 1, lo, :] = dot(t00, part(0, lo), NN) + dot(t01, part(0, hi), NN)
        acc[h, 1, hi, :] = dot(t11, part(0, hi), NN)
        b00, b01, b11 = scores(1, 0, lo, upp, hi)
        acc[h, 2, lo, :] = dot(b00, part(3, lo), NN) + dot(b01, part(3, hi), NN)
        acc[h, 2, hi, :] = dot(b11, part(3, hi), NN)

    def finish(h, ks, qs):
        at = pl.ds(pl.multiple_of(h * HD, HD), HD)
        gq_out[0, :, at] = (factor * (acc[h, 0] + dot(xin[h, 3], ks, NT))).astype(jnp.bfloat16)
        gk_out[0, :, at] = (factor * (acc[h, 1] + dot(xin[h, 2], qs, NT))).astype(jnp.bfloat16)
        gv_out[0, :, at] = (factor * (acc[h, 2] + dot(xin[h, 1], qs, NN))).astype(jnp.bfloat16)

    def finish_normal(h):
        wait_bytes(st.at[h, 0 : row - 1], c_recv.at[h])
        ks = st[h, 0 : row // 2].reshape(HD, HD)
        qs = st[h, row // 2 : row].reshape(HD, HD)
        finish(h, ks, qs)

    def finish_early(h):
        e = h - normal
        wait_bytes(mate.at[0, e], m_recv.at[e])
        late = mate[1, e]
        ks = est[0, :, e].reshape(HD, HD) + jnp.where(core == 1, late, 0.0)
        qs = est[1, :, e].reshape(HD, HD) + jnp.where(core == 0, late, 0.0)
        finish(h, ks.astype(jnp.bfloat16), qs.astype(jnp.bfloat16))

    def wait_round(r):
        pl.semaphore_wait(rounds.at[r], line_count(2**r))

    for h in range(BEFORE):
        send_y(h)

    @pl.when(core == 1)
    def _():
        pl.semaphore_wait(reply.at[0], 1)

    early_rows()
    early_parts()
    for h in range(BEFORE, BETWEEN):
        send_y(h)

    @pl.when(z + 1 < nz)
    def _():
        pl.semaphore_wait(reply.at[1], 1)

    @pl.when(x + 1 < nx)
    def _():
        pl.semaphore_wait(reply.at[2], 1)

    signal_line(rounds.at[0], 1)
    early_merge()
    for h in range(BETWEEN, min(WINDOW, heads)):
        send_y(h)
    for r in range(rounds.shape[0]):
        wait_round(r)
        if r + 1 < rounds.shape[0]:
            signal_line(rounds.at[r + 1], 2 ** (r + 1))

    @pl.loop(0, heads)
    def _(h):
        @pl.when(h + WINDOW < heads)
        def _():
            send_y(h + WINDOW)

        wait_y(h)

        @pl.when(h < normal)
        def _():
            states(h)

        @pl.when(h >= normal)
        def _():
            late_state(h)

        def lagged(lag, first, end, fn):
            @pl.when((h - lag >= first) & (h - lag < end))
            def _():
                fn(h - lag)

        def at(step, fn):
            @pl.when(h == step)
            def _():
                fn()

        at(AT_SUM, early_sum)
        lagged(LAG_PREFIX, 0, normal, prefixes)
        lagged(LAG_TOTAL, BUSY, normal, totals)
        causal(h)
        lagged(LAG_TOTAL, 0, BUSY, totals)
        at(AT_TOTAL, early_totals)
        at(AT_PREFIX, early_prefixes)
        lagged(LAG_FINISH, 0, normal, finish_normal)
        at(AT_SHARE, early_share)

        @pl.when(h == AT_FINISH)
        def _():
            wait_bytes(est.at[0], ed_recv)

            @pl.loop(normal, AT_FINISH + 1)
            def _(g):
                finish_early(g)

        @pl.when(h > AT_FINISH)
        def _():
            finish_early(h)

    wait_bytes(ear.at[0], e_send)
    wait_bytes(phop, h_send)
    wait_bytes(precv, p_send)
    wait_bytes(egat.at[0 : nz - 1], ea_send)
    wait_bytes(etot.at[0 : nx - 1], eb_send)
    wait_bytes(est.at[0, 0 : nz - 1], ec_send)
    wait_bytes(est.at[0], ed_send)

    @pl.loop(0, heads)
    def _(h):
        wait_bytes(xin.at[h, 0 : ny - 1], y_send.at[h])

    @pl.loop(0, normal)
    def _(h):
        wait_bytes(gat.at[h, 0 : row - 1], a_send.at[h])
        wait_bytes(tot.at[h, 0 : nx - 1], b_send.at[h])
        wait_bytes(st.at[h, 0 : row - 1], c_send.at[h])

    @pl.loop(0, early)
    def _(e):
        wait_bytes(mate.at[0, e], m_send.at[e])


def store(gq_in, gk_in, gv_in, gq_out, gk_out, gv_out, sems):
    pairs = ((gq_in, gq_out), (gk_in, gk_out), (gv_in, gv_out))
    copies = []
    for i, (src, dst) in enumerate(pairs):
        for j in range(sems.shape[1]):
            at = pl.ds(j * (BLOCK // sems.shape[1]), BLOCK // sems.shape[1])
            copies.append(pltpu.make_async_copy(src.at[0, at, :], dst.at[0, at, :], sems.at[i, j]))
    for copy in copies:
        copy.start()
    for copy in copies:
        copy.wait()


def shards(nx, query, keys, values, grad_out):
    ny = lax.axis_size("head")
    nctx = lax.axis_size("ctx")
    row = nctx // nx
    nz = row // 2
    heads = query.shape[2] // ny // HD
    factor = (HD * BLOCK * nctx) ** (-0.5)
    per = 2 * HD // row
    early = min(EARLY, heads - 1)
    normal = heads - early
    dma = pltpu.SemaphoreType.DMA
    flops = heads * (9 * 2 * BLOCK * BLOCK * HD * 3 // 4 + 5 * 2 * BLOCK * HD * HD)
    ins = [pltpu.with_memory_space_constraint(a, pltpu.HBM) for a in (query, keys, values, grad_out)]
    f32, bf16 = jnp.float32, jnp.bfloat16
    grads = pl.pallas_call(
        functools.partial(kernel, heads, nx, row, factor),
        out_shape=[pltpu.VMEM((1, BLOCK, heads * HD), bf16)] * 3,
        in_specs=[pl.BlockSpec(memory_space=pltpu.HBM)] * 4,
        out_specs=[pl.BlockSpec(memory_space=pltpu.VMEM)] * 3,
        scratch_shapes=[
            pltpu.VMEM((heads, 4, BLOCK, HD), bf16),
            pltpu.VMEM((heads, 3, BLOCK, HD), f32),
            pltpu.VMEM((normal, 2 * HD, HD), f32),
            pltpu.VMEM((normal, row, per, HD), f32),
            pltpu.VMEM((normal, nx, per, HD), f32),
            pltpu.VMEM((normal, row, per, HD), bf16),
            pltpu.VMEM((normal, row, per, HD), bf16),
            pltpu.VMEM((2, ny, 2 * BLOCK // ny, early * HD), bf16),
            pltpu.VMEM((6, early, HD // 2, HD), bf16),
            pltpu.VMEM((2, early, HD // 2, HD), f32),
            pltpu.VMEM((2, early, HD // 2, HD), bf16),
            pltpu.VMEM((2, 2, early, HD // 2, HD), bf16),
            pltpu.VMEM((nz, early, per, HD), f32),
            pltpu.VMEM((nz, early, per, HD), f32),
            pltpu.VMEM((nx, early, per, HD), f32),
            pltpu.VMEM((nz, early, per, HD), f32),
            pltpu.VMEM((2, nz, early, per, HD), f32),
            pltpu.VMEM((2, early, HD, HD), f32),
            pltpu.SemaphoreType.REGULAR(((nz - 1).bit_length(),)),
            pltpu.SemaphoreType.REGULAR((3,)),
        ]
        + [dma((heads,))] * 3
        + [dma((normal,))] * 6
        + [dma((early,))] * 2
        + [dma] * 15,
        compiler_params=pltpu.CompilerParams(
            collective_id=1, has_side_effects=True, vmem_limit_bytes=44 * 2**20
        ),
        cost_estimate=pl.CostEstimate(flops=flops, bytes_accessed=8 * 2**20, transcendentals=0),
    )(*ins)
    return pl.pallas_call(
        store,
        out_shape=[jax.ShapeDtypeStruct(a.shape, a.dtype) for a in grads],
        in_specs=[pl.BlockSpec(memory_space=pltpu.VMEM)] * 3,
        out_specs=[pl.BlockSpec(memory_space=pltpu.HBM)] * 3,
        scratch_shapes=[dma((3, PIECES))],
    )(*[pltpu.with_memory_space_constraint(a, pltpu.VMEM) for a in grads])


def solution(mesh):
    nx = 4
    in_specs = (P("ctx", "head", None),) * 4
    out_specs = (P("ctx", None, "head"),) * 3
    return jax.shard_map(
        functools.partial(shards, nx), mesh=mesh, in_specs=in_specs, out_specs=out_specs, check_vma=False
    )
```

```python
import functools

import jax
import jax.numpy as jnp
from jax import lax
from jax.experimental import pallas as pl
from jax.experimental.pallas import tpu as pltpu
from jax.sharding import PartitionSpec as P

HD = 128
BLOCK = 512
HALF = 256
MESH = pl.DeviceIdType.MESH
NT = (((1,), (1,)), ((), ()))
NN = (((1,), (0,)), ((), ()))
TN = (((0,), (0,)), ((), ()))
WINDOW = 6
BEFORE = 1
BETWEEN = 2
BUSY = 3
PIECES = 2
EARLY = 4
AT_SUM, AT_TOTAL, AT_PREFIX, AT_SHARE, AT_FINISH = 1, 2, 3, 5, 6
LAG_TOTAL, LAG_PREFIX, LAG_FINISH = 1, 2, 4


def dot(a, b, dims):
    return lax.dot_general(a, b, dims, preferred_element_type=jnp.float32)


def kernel(
    heads, nx, row, factor,
    q_in, k_in, v_in, g_in, gq_out, gk_out, gv_out,
    xin, acc, own, gat, tot, pre, st,
    ear, psend, pkeep, phop, precv, chip, egat, etot, epre, est, mate,
    rounds, reply, y_send, y_recv, y_loc, a_send, a_recv, b_send, b_recv, c_send, c_recv,
    m_send, m_recv, e_loc, e_send, e_recv, h_send, h_recv, p_send, p_recv,
    ea_send, ea_recv, eb_send, eb_recv, ec_send, ec_recv, ed_send, ed_recv,
):
    ny = lax.axis_size("head")
    y = lax.axis_index("head")
    ctx = lax.axis_index("ctx")
    nz = row // 2
    x = ctx // row
    me = ctx % row
    z = me // 2
    core = me % 2
    is_q = me // nz
    rows_y = BLOCK // ny
    ins = (q_in, k_in, v_in, g_in)
    per = 2 * HD // row
    early = ear.shape[3] // HD
    normal = heads - early
    dists = (2, 1, 3)

    row_order = sorted(range(1, row), key=lambda d: -min(d, row - d))
    z_order = sorted(range(1, nz), key=lambda d: -min(d, nz - d))
    x_order = sorted(range(1, nx), key=lambda d: -min(d, nx - d))

    def y_peer(d):
        return {"head": lax.rem(y + d, ny)}

    def place(x_at, z_at, core_at):
        return {"ctx": (x_at * nz + z_at) * 2 + core_at}

    def row_peer(d):
        t = lax.rem(me + d, row)
        return t, {"ctx": x * row + t}

    def x_peer(d):
        return {"ctx": lax.rem(x + d, nx) * row + me}

    partner = place(x, z, 1 - core)

    def signal(sem, device):
        pl.semaphore_signal(sem, inc=1, device_id=device, device_id_type=MESH)

    def signal_line(sem, step):
        @pl.when(z >= step)
        def _():
            signal(sem, place(x, z - step, core))

        @pl.when(z + step < nz)
        def _():
            signal(sem, place(x, z + step, core))

        if step < nx:
            @pl.when(x >= step)
            def _():
                signal(sem, place(x - step, z, core))

            @pl.when(x + step < nx)
            def _():
                signal(sem, place(x + step, z, core))

    def line_count(step):
        count = lax.min(z // step, 1) + lax.min((nz - 1 - z) // step, 1)
        return count + lax.min(x // step, 1) + lax.min((nx - 1 - x) // step, 1)

    barrier = pltpu.get_barrier_semaphore()
    for d in dists:
        signal(barrier, y_peer(d))

    @pl.when(core == 1)
    def _():
        signal(barrier, partner)

    @pl.when(z + 1 < nz)
    def _():
        signal(barrier, place(x, z + 1, core))

    @pl.when(x + 1 < nx)
    def _():
        signal(barrier, place(x + 1, z, core))

    pl.semaphore_wait(barrier, ny - 1 + (1 - core) + lax.min(z, 1) + lax.min(x, 1))

    def remote(src, dst, send, recv, device):
        pltpu.make_async_remote_copy(
            src_ref=src, dst_ref=dst, send_sem=send, recv_sem=recv,
            device_id=device, device_id_type=MESH,
        ).start()

    def wait_bytes(ref, sem):
        pltpu.make_async_copy(ref, ref, sem).wait()

    def my_rows(owner):
        return pl.ds(pl.multiple_of(owner * rows_y, rows_y), rows_y)

    def cols(owner, h, count=1):
        return pl.ds(pl.multiple_of((owner * heads + h) * HD, HD), count * HD)

    def send_y(h):
        for d in dists:
            tgt = lax.rem(y + d, ny)
            for a in range(4):
                remote(
                    ins[a].at[0, :, cols(tgt, h)], xin.at[h, a, my_rows(y), :],
                    y_send.at[h], y_recv.at[h], {"head": tgt},
                )
        for a in range(4):
            pltpu.make_async_copy(
                ins[a].at[0, :, cols(y, h)], xin.at[h, a, my_rows(y), :], y_loc.at[h]
            ).start()

    def early_rows():
        at = pl.ds(pl.multiple_of(core * rows_y, rows_y), rows_y)
        keys_side, query_side = (k_in, v_in), (q_in, g_in)

        def go(keep, give):
            for t in range(ny):
                for i in range(2):
                    src = (0, slice(None), cols(t, normal, early))
                    dst = ear.at[i, t, at, :]
                    remote(give[i].at[src], dst, e_send, e_recv, partner)
                    pltpu.make_async_copy(keep[i].at[src], dst, e_loc).start()

        @pl.when(core == 0)
        def _():
            go(keys_side, query_side)

        @pl.when(core == 1)
        def _():
            go(query_side, keys_side)

    def early_parts():
        wait_bytes(ear.at[0], e_loc)
        wait_bytes(ear.at[0], e_recv)
        top, low = slice(0, HD // 2), slice(HD // 2, HD)
        for d in (2, 1, 3, 0):
            t = lax.rem(y + d, ny)
            for e in range(early):
                at = slice(e * HD, (e + 1) * HD)
                part = dot(ear[0, t, :, at], ear[1, t, :, at], TN)
                if d == 0:
                    chip[:, e] = part.reshape(nz, per, HD)
                elif d == 2:
                    psend[0, e] = part[top].astype(jnp.bfloat16)
                    psend[1, e] = part[low].astype(jnp.bfloat16)
                elif d == 1:
                    psend[2, e] = part[top].astype(jnp.bfloat16)
                    pkeep[0, e] = part[low]
                else:
                    psend[3, e] = part[low].astype(jnp.bfloat16)
                    pkeep[1, e] = part[top]
            if d == 2:
                remote(psend.at[0], phop.at[0], h_send, h_recv, y_peer(ny - 1))
                remote(psend.at[1], phop.at[1], h_send, h_recv, y_peer(1))
            elif d == 1:
                remote(psend.at[2], precv.at[0, 0], p_send, p_recv, y_peer(1))
            elif d == 3:
                remote(psend.at[3], precv.at[1, 1], p_send, p_recv, y_peer(ny - 1))

    def early_merge():
        wait_bytes(phop, h_recv)
        for e in range(early):
            psend[4, e] = (pkeep[0, e] + phop[1, e].astype(jnp.float32)).astype(jnp.bfloat16)
            psend[5, e] = (pkeep[1, e] + phop[0, e].astype(jnp.float32)).astype(jnp.bfloat16)
        remote(psend.at[4], precv.at[0, 1], p_send, p_recv, y_peer(1))
        remote(psend.at[5], precv.at[1, 0], p_send, p_recv, y_peer(ny - 1))

    def early_sum():
        wait_bytes(precv, p_recv)
        half = nz // 2
        for e in range(early):
            for i in range(2):
                at = slice(i * half, (i + 1) * half)
                got = precv[0, i, e].astype(jnp.float32) + precv[1, i, e].astype(jnp.float32)
                chip[at, e] = chip[at, e] + got.reshape(half, per, HD)
        for d in z_order:
            t = lax.rem(z + d, nz)
            remote(chip.at[t], egat.at[z], ea_send, ea_recv, place(x, t, core))
        egat[z] = chip[z]

    def early_totals():
        wait_bytes(egat.at[0 : nz - 1], ea_recv)
        total = egat[0]
        for s in range(1, nz):
            total = total + egat[s]
        etot[x] = total
        for d in x_order:
            remote(etot.at[x], etot.at[x], eb_send, eb_recv, x_peer(d))

    def base(parts, x_side):
        run = jnp.zeros(parts.shape[1:], jnp.float32)
        for s in range(nx):
            run = run + jnp.where((s - x) * x_side > 0, parts[s], 0.0)
        return run

    def early_prefixes():
        wait_bytes(etot.at[0 : nx - 1], eb_recv)
        run = base(etot, 2 * core - 1)
        for s in range(nz):
            at = s + core * (nz - 1 - 2 * s)
            epre[at] = run
            run = run + egat[at]
        for d in z_order:
            t = lax.rem(z + d, nz)
            remote(epre.at[t], est.at[core, z], ec_send, ec_recv, place(x, t, core))
        est[core, z] = epre[z]

    def early_share():
        wait_bytes(est.at[0, 0 : nz - 1], ec_recv)
        remote(est.at[core], est.at[core], ed_send, ed_recv, partner)

    def wait_y(h):
        wait_bytes(xin.at[h, 0 : ny - 1], y_recv.at[h])
        wait_bytes(xin.at[h, 0:1], y_loc.at[h])

    def states(h):
        own[h, 0:HD, :] = dot(xin[h, 1], xin[h, 2], TN)
        own[h, HD : 2 * HD, :] = dot(xin[h, 0], xin[h, 3], TN)
        for d in row_order:
            t, peer = row_peer(d)
            src = own.at[h, pl.ds(pl.multiple_of(t * per, per), per), :]
            remote(src, gat.at[h, me], a_send.at[h], a_recv.at[h], peer)
        gat[h, me] = own[h, pl.ds(pl.multiple_of(me * per, per), per), :]

    def late_state(h):
        e = h - normal
        mate[0, e] = dot(xin[h, 1 - core], xin[h, 2 + core], TN)
        remote(mate.at[0, e], mate.at[1, e], m_send.at[e], m_recv.at[e], partner)

    def totals(h):
        wait_bytes(gat.at[h, 0 : row - 1], a_recv.at[h])
        total = gat[h, 0]
        for s in range(1, row):
            total = total + gat[h, s]
        tot[h, x] = total
        for d in x_order:
            remote(tot.at[h, x], tot.at[h, x], b_send.at[h], b_recv.at[h], x_peer(d))

    def prefixes(h):
        wait_bytes(tot.at[h, 0 : nx - 1], b_recv.at[h])
        run = base(tot.at[h], 2 * is_q - 1)
        for s in range(row):
            at = s + is_q * (row - 1 - 2 * s)
            pre[h, at] = run.astype(jnp.bfloat16)
            run = run + gat[h, at]
        for d in row_order:
            t, peer = row_peer(d)
            remote(pre.at[h, t], st.at[h, me], c_send.at[h], c_recv.at[h], peer)
        st[h, me] = pre[h, me]

    r_at = lax.broadcasted_iota(jnp.int32, (HALF, HALF), 0)
    c_at = lax.broadcasted_iota(jnp.int32, (HALF, HALF), 1)

    def causal(h):
        lo, hi = pl.ds(0, HALF), pl.ds(HALF, HALF)

        def low(s):
            return jnp.where(r_at >= c_at, s, 0.0).astype(jnp.bfloat16)

        def upp(s):
            return jnp.where(r_at <= c_at, s, 0.0).astype(jnp.bfloat16)

        def part(a, at):
            return xin[h, a, at, :]

        def scores(left, right, first, other, last):
            s_first = dot(part(left, lo), part(right, lo), NT)
            s_last = dot(part(left, hi), part(right, hi), NT)
            s_other = dot(part(left, first), part(right, last), NT)
            return other(s_first), s_other.astype(jnp.bfloat16), other(s_last)

        a00, a10, a11 = scores(3, 2, hi, low, lo)
        acc[h, 0, lo, :] = dot(a00, part(1, lo), NN)
        acc[h, 0, hi, :] = dot(a10, part(1, lo), NN) + dot(a11, part(1, hi), NN)
        t00, t01, t11 = scores(2, 3, lo, upp, hi)
        acc[h, 1, lo, :] = dot(t00, part(0, lo), NN) + dot(t01, part(0, hi), NN)
        acc[h, 1, hi, :] = dot(t11, part(0, hi), NN)
        b00, b01, b11 = scores(1, 0, lo, upp, hi)
        acc[h, 2, lo, :] = dot(b00, part(3, lo), NN) + dot(b01, part(3, hi), NN)
        acc[h, 2, hi, :] = dot(b11, part(3, hi), NN)

    def finish(h, ks, qs):
        at = pl.ds(pl.multiple_of(h * HD, HD), HD)
        gq_out[0, :, at] = (factor * (acc[h, 0] + dot(xin[h, 3], ks, NT))).astype(jnp.bfloat16)
        gk_out[0, :, at] = (factor * (acc[h, 1] + dot(xin[h, 2], qs, NT))).astype(jnp.bfloat16)
        gv_out[0, :, at] = (factor * (acc[h, 2] + dot(xin[h, 1], qs, NN))).astype(jnp.bfloat16)

    def finish_normal(h):
        wait_bytes(st.at[h, 0 : row - 1], c_recv.at[h])
        ks = st[h, 0 : row // 2].reshape(HD, HD)
        qs = st[h, row // 2 : row].reshape(HD, HD)
        finish(h, ks, qs)

    def finish_early(h):
        e = h - normal
        wait_bytes(mate.at[0, e], m_recv.at[e])
        late = mate[1, e]
        ks = est[0, :, e].reshape(HD, HD) + jnp.where(core == 1, late, 0.0)
        qs = est[1, :, e].reshape(HD, HD) + jnp.where(core == 0, late, 0.0)
        finish(h, ks.astype(jnp.bfloat16), qs.astype(jnp.bfloat16))

    def wait_round(r):
        pl.semaphore_wait(rounds.at[r], line_count(2**r))

    for h in range(BEFORE):
        send_y(h)

    @pl.when(core == 0)
    def _():
        signal(reply.at[0], partner)

    @pl.when(z >= 1)
    def _():
        signal(reply.at[1], place(x, z - 1, core))

    @pl.when(x >= 1)
    def _():
        signal(reply.at[2], place(x - 1, z, core))

    @pl.when(core == 1)
    def _():
        pl.semaphore_wait(reply.at[0], 1)

    early_rows()
    early_parts()
    for h in range(BEFORE, BETWEEN):
        send_y(h)

    @pl.when(z + 1 < nz)
    def _():
        pl.semaphore_wait(reply.at[1], 1)

    @pl.when(x + 1 < nx)
    def _():
        pl.semaphore_wait(reply.at[2], 1)

    signal_line(rounds.at[0], 1)
    early_merge()
    for h in range(BETWEEN, min(WINDOW, heads)):
        send_y(h)
    for r in range(rounds.shape[0]):
        wait_round(r)
        if r + 1 < rounds.shape[0]:
            signal_line(rounds.at[r + 1], 2 ** (r + 1))

    @pl.loop(0, heads)
    def _(h):
        @pl.when(h + WINDOW < heads)
        def _():
            send_y(h + WINDOW)

        wait_y(h)

        @pl.when(h < normal)
        def _():
            states(h)

        @pl.when(h >= normal)
        def _():
            late_state(h)

        def lagged(lag, first, end, fn):
            @pl.when((h - lag >= first) & (h - lag < end))
            def _():
                fn(h - lag)

        def at(step, fn):
            @pl.when(h == step)
            def _():
                fn()

        at(AT_SUM, early_sum)
        lagged(LAG_PREFIX, 0, normal, prefixes)
        lagged(LAG_TOTAL, BUSY, normal, totals)
        causal(h)
        lagged(LAG_TOTAL, 0, BUSY, totals)
        at(AT_TOTAL, early_totals)
        at(AT_PREFIX, early_prefixes)
        lagged(LAG_FINISH, 0, normal, finish_normal)
        at(AT_SHARE, early_share)

        @pl.when(h == AT_FINISH)
        def _():
            wait_bytes(est.at[0], ed_recv)

            @pl.loop(normal, AT_FINISH + 1)
            def _(g):
                finish_early(g)

        @pl.when(h > AT_FINISH)
        def _():
            finish_early(h)

    wait_bytes(ear.at[0], e_send)
    wait_bytes(phop, h_send)
    wait_bytes(precv, p_send)
    wait_bytes(egat.at[0 : nz - 1], ea_send)
    wait_bytes(etot.at[0 : nx - 1], eb_send)
    wait_bytes(est.at[0, 0 : nz - 1], ec_send)
    wait_bytes(est.at[0], ed_send)

    @pl.loop(0, heads)
    def _(h):
        wait_bytes(xin.at[h, 0 : ny - 1], y_send.at[h])

    @pl.loop(0, normal)
    def _(h):
        wait_bytes(gat.at[h, 0 : row - 1], a_send.at[h])
        wait_bytes(tot.at[h, 0 : nx - 1], b_send.at[h])
        wait_bytes(st.at[h, 0 : row - 1], c_send.at[h])

    @pl.loop(0, early)
    def _(e):
        wait_bytes(mate.at[0, e], m_send.at[e])


def store(gq_in, gk_in, gv_in, gq_out, gk_out, gv_out, sems):
    pairs = ((gq_in, gq_out), (gk_in, gk_out), (gv_in, gv_out))
    copies = []
    for i, (src, dst) in enumerate(pairs):
        for j in range(sems.shape[1]):
            at = pl.ds(j * (BLOCK // sems.shape[1]), BLOCK // sems.shape[1])
            copies.append(pltpu.make_async_copy(src.at[0, at, :], dst.at[0, at, :], sems.at[i, j]))
    for copy in copies:
        copy.start()
    for copy in copies:
        copy.wait()


def shards(nx, query, keys, values, grad_out):
    ny = lax.axis_size("head")
    nctx = lax.axis_size("ctx")
    row = nctx // nx
    nz = row // 2
    heads = query.shape[2] // ny // HD
    factor = (HD * BLOCK * nctx) ** (-0.5)
    per = 2 * HD // row
    early = min(EARLY, heads - 1)
    normal = heads - early
    dma = pltpu.SemaphoreType.DMA
    flops = heads * (9 * 2 * BLOCK * BLOCK * HD * 3 // 4 + 5 * 2 * BLOCK * HD * HD)
    ins = [pltpu.with_memory_space_constraint(a, pltpu.HBM) for a in (query, keys, values, grad_out)]
    f32, bf16 = jnp.float32, jnp.bfloat16
    grads = pl.pallas_call(
        functools.partial(kernel, heads, nx, row, factor),
        out_shape=[pltpu.VMEM((1, BLOCK, heads * HD), bf16)] * 3,
        in_specs=[pl.BlockSpec(memory_space=pltpu.HBM)] * 4,
        out_specs=[pl.BlockSpec(memory_space=pltpu.VMEM)] * 3,
        scratch_shapes=[
            pltpu.VMEM((heads, 4, BLOCK, HD), bf16),
            pltpu.VMEM((heads, 3, BLOCK, HD), f32),
            pltpu.VMEM((normal, 2 * HD, HD), f32),
            pltpu.VMEM((normal, row, per, HD), f32),
            pltpu.VMEM((normal, nx, per, HD), f32),
            pltpu.VMEM((normal, row, per, HD), bf16),
            pltpu.VMEM((normal, row, per, HD), bf16),
            pltpu.VMEM((2, ny, 2 * BLOCK // ny, early * HD), bf16),
            pltpu.VMEM((6, early, HD // 2, HD), bf16),
            pltpu.VMEM((2, early, HD // 2, HD), f32),
            pltpu.VMEM((2, early, HD // 2, HD), bf16),
            pltpu.VMEM((2, 2, early, HD // 2, HD), bf16),
            pltpu.VMEM((nz, early, per, HD), f32),
            pltpu.VMEM((nz, early, per, HD), f32),
            pltpu.VMEM((nx, early, per, HD), f32),
            pltpu.VMEM((nz, early, per, HD), f32),
            pltpu.VMEM((2, nz, early, per, HD), f32),
            pltpu.VMEM((2, early, HD, HD), f32),
            pltpu.SemaphoreType.REGULAR(((nz - 1).bit_length(),)),
            pltpu.SemaphoreType.REGULAR((3,)),
        ]
        + [dma((heads,))] * 3
        + [dma((normal,))] * 6
        + [dma((early,))] * 2
        + [dma] * 15,
        compiler_params=pltpu.CompilerParams(
            collective_id=1, has_side_effects=True, vmem_limit_bytes=44 * 2**20
        ),
        cost_estimate=pl.CostEstimate(flops=flops, bytes_accessed=8 * 2**20, transcendentals=0),
    )(*ins)
    return pl.pallas_call(
        store,
        out_shape=[jax.ShapeDtypeStruct(a.shape, a.dtype) for a in grads],
        in_specs=[pl.BlockSpec(memory_space=pltpu.VMEM)] * 3,
        out_specs=[pl.BlockSpec(memory_space=pltpu.HBM)] * 3,
        scratch_shapes=[dma((3, PIECES))],
    )(*[pltpu.with_memory_space_constraint(a, pltpu.VMEM) for a in grads])


def solution(mesh):
    nx = 4
    in_specs = (P("ctx", "head", None),) * 4
    out_specs = (P("ctx", None, "head"),) * 3
    return jax.shard_map(
        functools.partial(shards, nx), mesh=mesh, in_specs=in_specs, out_specs=out_specs, check_vma=False
    )
```
